512 devices in a mesh: row: 8 (over z_hi, x), col: 8 (over z_lo), layer: 8 (over y, core).
Axes of the slice: x: 4, y: 4, z: 16 (z_hi: 2, z_lo: 8; z = z_hi * 8 + z_lo), core: 2. Of those that a mesh axis runs over, the one named last changes fastest.
Arguments:
- blocks: float32 [128, 8, 3, 96, 96], P(('row', 'layer'), 'col'), may hold values from -2.4 to 2.4
- block_cols: int32 [128, 8, 3], replicated, may hold values from 0 to 15, as said below
- occupancy: int32 [128, 8, 3], replicated, may hold values from 0 to 1, as said below
Outputs:
- product: float32 [128, 8, 3, 96, 96], P(('row', 'layer'), 'col')
- trace: float32 [], replicated
The draws below stay inside these ranges and needn't reach their ends.
Inputs may be any that keep to these rules, and one draw needn't show every extreme that they name: `block_cols`: within one block row and column group the 3 block columns are distinct; for block row I the column group I // 16 holds I % 16 in slot 0. `occupancy`: slot 0 of block row I in column group I // 16 is always 1.
All inputs are finite; a program needn't handle non-finite values.
Results may differ from the reference program's by a relative error of at most 0.0003.
Values sent between devices are 32-bit elements; how exact they have to be, the bound alone decides.
A program may use at most 64 MiB of HBM per device.

```python
import jax
import jax.numpy as jnp
from jax import lax

B = 96
RMAX = 3
NB = 128
GCOLS = 16
N_COL = 8


def draw_block_cols(key, part):
    key = jax.random.fold_in(key, 11)
    noise = jax.random.randint(key, (NB, N_COL, GCOLS), 0, 2 ** 20)
    column = jnp.arange(GCOLS, dtype=jnp.int32)[None, None, :]
    rows = jnp.arange(NB, dtype=jnp.int32)[:, None, None]
    group = jnp.arange(N_COL, dtype=jnp.int32)[None, :, None]
    diagonal = ((group == rows // GCOLS) & (column == rows % GCOLS)).astype(jnp.int32)
    score = noise * GCOLS + column + diagonal * 2 ** 28
    values, picked = lax.top_k(score, RMAX)
    return picked.astype(jnp.int32)


def draw_occupancy(key, part):
    key = jax.random.fold_in(key, 23)
    base = jax.random.randint(key, (NB, N_COL, RMAX), 0, 2)
    rows = jnp.arange(NB, dtype=jnp.int32)[:, None, None]
    group = jnp.arange(N_COL, dtype=jnp.int32)[None, :, None]
    slot = jnp.arange(RMAX, dtype=jnp.int32)[None, None, :]
    forced = ((group == rows // GCOLS) & (slot == 0)).astype(jnp.int32)
    return jnp.maximum(base, forced).astype(jnp.int32)


def shard_levels(own_key, shape, cuts, least, top_value):
    loudness, own = 1.0, jax.random.fold_in(own_key, 6)
    for axis_at, parts in cuts:
        steps = jnp.exp(jax.random.uniform(jax.random.fold_in(own, axis_at), (parts,), jnp.float32, least / len(cuts), top_value / len(cuts)))
        loudness = loudness * jnp.repeat(steps, shape[axis_at] // parts).reshape([-1 if axis == axis_at else 1 for axis in range(len(shape))])
    return loudness


def bell_draw(stream_key, extent, deviation, reach, split=(), held_as=jnp.bfloat16):
    level = shard_levels(stream_key, extent, split, -0.22, 0.18) if split else 1.0
    drawn = jax.random.normal(stream_key, extent, jnp.float32) * deviation * level
    return jnp.minimum(jnp.maximum(drawn, -reach), reach).astype(held_as)


def setup_inputs(seed: int = 0) -> dict:
    seeds = jax.random.split(jax.random.key(seed), 4)
    return {
        "blocks": bell_draw(seeds[0], (NB, N_COL, RMAX, B, B), 0.3, 2.4, ((0, 64), (1, 8)), jnp.float32),
        "block_cols": draw_block_cols(jax.random.fold_in(seeds[3], 71), 0),
        "occupancy": draw_occupancy(jax.random.fold_in(seeds[3], 71), 0),
    }


def reference(blocks, block_cols, occupancy):
    count = blocks.shape[0]
    groups = blocks.shape[1]
    width = count // groups
    occ_float = occupancy.astype(jnp.float32)
    group_ids = jnp.arange(groups, dtype=jnp.int32)

    def one_row(index):
        row_blocks = blocks[index]
        row_cols = block_cols[index]
        row_occ = occ_float[index]
        inner = (group_ids[:, None] * width + row_cols).astype(jnp.int32)
        gathered = blocks[inner]
        inner_cols = block_cols[inner]
        inner_occ = occ_float[inner]
        match = (inner_cols[:, :, :, :, None] == row_cols[None, None, :, None, :]).astype(jnp.float32)
        match = match * inner_occ[:, :, :, :, None] * row_occ[:, :, None, None, None]
        combined = jnp.einsum('gtcus,gtcubd->gtcsbd', match, gathered, precision=lax.Precision.HIGHEST)
        result = jnp.einsum('gtab,gtcsbd->csad', row_blocks, combined, precision=lax.Precision.HIGHEST)
        return result * row_occ[:, :, None, None]

    product = lax.map(one_row, jnp.arange(count, dtype=jnp.int32))
    rows = jnp.arange(count, dtype=jnp.int32)[:, None, None]
    global_cols = group_ids[None, :, None] * width + block_cols
    diagonal = (global_cols == rows).astype(jnp.float32) * occ_float
    traces = jnp.trace(product, axis1=3, axis2=4)
    return product, jnp.sum(diagonal * traces)
```

```python
import functools

import jax
import jax.numpy as jnp
from jax import lax
from jax.experimental import pallas as pl
from jax.experimental.pallas import tpu as pltpu
from jax.sharding import PartitionSpec as P

MESH = pl.DeviceIdType.MESH
NX, NY, NZH, NZL, NK = 4, 4, 2, 8, 2
B, SLOTS, PACK = 96, 3, 72
HALF = SLOTS * PACK
LO = 104
NB, GROUPS, WIDTH = 128, 8, 16
MAXHIT = 2 * GROUPS * SLOTS * SLOTS


def here():
    r, c, l = lax.axis_index("row"), lax.axis_index("col"), lax.axis_index("layer")
    return {"x": r % NX, "zh": r // NX, "zl": c, "y": l // NK, "k": l % NK}


def device(at):
    return {"row": at["zh"] * NX + at["x"], "col": at["zl"], "layer": at["y"] * NK + at["k"]}


def moved(at, axis, by):
    at = dict(at)
    if axis == "x":
        at["x"] = (at["x"] + by + NX) % NX
    elif axis == "y":
        at["y"] = (at["y"] + by + NY) % NY
    elif axis == "k":
        at["k"] = 1 - at["k"]
    else:
        z = (at["zh"] * NZL + at["zl"] + by + NZH * NZL) % (NZH * NZL)
        at["zh"], at["zl"] = z // NZL, z % NZL
    return at


def pack(block):
    rest = block[PACK:, :]
    side = jnp.concatenate([rest[:, 0:32], rest[:, 32:64], rest[:, 64:96]], axis=0)
    return jnp.concatenate([block[:PACK, :], side], axis=1)


def unpack(packed):
    side = packed[:, B:]
    rest = jnp.concatenate([side[0:24], side[24:48], side[48:72]], axis=1)
    return jnp.concatenate([packed[:, :B], rest], axis=0)


def gather_kernel(b_ref, left_ref, right_ref, own, lsem, psem, csem, xsem, dsem):
    me = here()
    zl, zh, x, y, k = me["zl"], me["zh"], me["x"], me["y"], me["k"]
    partners = [moved(me, "z", 1), moved(me, "z", -1), moved(me, "z", 8), moved(me, "x", 1), moved(me, "x", -1),
                moved(me, "y", 1), moved(me, "y", -1), moved(me, "k", 1)]
    barrier = pltpu.get_barrier_semaphore()
    for other in partners:
        pl.semaphore_signal(barrier, inc=1, device_id=device(other), device_id_type=MESH)
    for i in range(2):
        for s in range(SLOTS):
            own[i, s * PACK:(s + 1) * PACK, :] = pack(b_ref[i, 0, s])
    local = [
        pltpu.make_async_copy(own, left_ref.at[zl], lsem.at[0]),
        pltpu.make_async_copy(own.at[0], right_ref.at[0, zh, k, x, y], lsem.at[1]),
        pltpu.make_async_copy(own.at[1], right_ref.at[1, zh, k, y, x], lsem.at[2]),
    ]
    for copy in local:
        copy.start()
    pl.semaphore_wait(barrier, len(partners))

    sent = []

    def send(src, dst, to, sems, index, when=None):
        copy = pltpu.make_async_remote_copy(
            src_ref=src, dst_ref=dst, send_sem=sems.at[(0,) + index], recv_sem=sems.at[(1,) + index],
            device_id=device(to), device_id_type=MESH)
        if when is None:
            copy.start()
        else:
            pl.when(when)(copy.start)
        sent.append((copy, when))
        return copy

    events = []

    far = moved(me, "z", 8)
    crossing = [
        send(own.at[0], right_ref.at[0, zh, k, x, y], far, csem, (0,)),
        send(own.at[1], right_ref.at[1, zh, k, y, x], far, csem, (1,)),
    ]

    line = {}

    def line_step(direction, n, part):
        to = moved(me, "z", direction)
        piece = jnp.clip(zl - direction * n, 0, NZL - 1)
        got = (zl >= n) if direction > 0 else (zl + n < NZL)
        more = (zl < NZL - 1) if direction > 0 else (zl > 0)
        slot = 0 if direction > 0 else 1
        if n > 0:
            pl.when(got)(line[direction, n - 1, part].wait_recv)
        if n < NZL - 1:
            src = own.at[part] if n == 0 else left_ref.at[piece, part]
            line[direction, n, part] = send(
                src, left_ref.at[piece, part], to, psem, (slot, n, part), jnp.logical_and(got, more))

    for part in range(2):
        for direction in (1, -1):
            line_step(direction, 0, part)
    for n in range(1, NZL):
        for part in range(2):
            for direction in (1, -1):
                events.append((5.0 * n + 2.5 * part, functools.partial(line_step, direction, n, part)))

    def plane(phase, half, start):
        first = ("x", "y")
        second = ("y", "x")
        size = {"x": NX, "y": NY}
        chunks = {}

        def ref(ab, p, q, rows=None):
            view = right_ref.at[ab, half, k, p, q]
            return view if rows is None else view.at[pl.ds(rows[0], rows[1])]

        lo, hi = (0, LO), (LO, HALF - LO)

        def spot(axis, by):
            return (me[axis] + by + size[axis]) % size[axis]

        def spread(ab, j):
            a, b = first[ab], second[ab]
            p, q = spot(a, j), me[b]
            for d, way in enumerate((1, -1)):
                chunks[ab, "b", j, d] = send(ref(ab, p, q), ref(ab, p, q), moved(me, b, way), xsem, (phase, ab, 4 + 4 * j + d))

        def begin(ab):
            a = first[ab]
            p, q = me[a], me[second[ab]]
            if phase == 1:
                crossing[ab].wait_recv()
            for d, way in enumerate((1, -1)):
                chunks[ab, "a", d] = send(ref(ab, p, q), ref(ab, p, q), moved(me, a, way), xsem, (phase, ab, d))
            spread(ab, 0)

        def pass_on(ab, d):
            way = 1 - 2 * d
            a = first[ab]
            p, q = spot(a, -way), me[second[ab]]
            chunks[ab, "a", d].wait_recv()
            rows = lo if d == 0 else hi
            chunks[ab, "a2", d] = send(ref(ab, p, q, rows), ref(ab, p, q, rows), moved(me, a, way), xsem, (phase, ab, 2 + d))
            spread(ab, 3 if way > 0 else 1)

        def opposite(ab):
            for d in range(2):
                chunks[ab, "a2", d].wait_recv()
            spread(ab, 2)

        def pass_second(ab, j):
            a, b = first[ab], second[ab]
            p = spot(a, j)
            for d, way in enumerate((1, -1)):
                q = spot(b, -way)
                chunks[ab, "b", j, d].wait_recv()
                rows = lo if d == 0 else hi
                chunks[ab, "b2", j, d] = send(ref(ab, p, q, rows), ref(ab, p, q, rows), moved(me, b, way), xsem, (phase, ab, 6 + 4 * j + d))

        def share(ab, j):
            for d in range(2):
                chunks[ab, "b2", j, d].wait_recv()
            p = spot(first[ab], j)
            src = right_ref.at[ab, half, k, p]
            chunks[ab, "c", j] = send(src, src, moved(me, "k", 1), dsem, (phase, ab, j))

        def finish(ab, j):
            chunks[ab, "c", j].wait_recv()

        order = [(0.0, begin)]
        for d in range(2):
            order.append((2.5, lambda ab, d=d: pass_on(ab, d)))
        order.append((6.0, lambda ab: pass_second(ab, 0)))
        order.append((7.0, lambda ab: opposite(ab)))
        order.append((10.0, lambda ab: pass_second(ab, 3)))
        order.append((11.0, lambda ab: share(ab, 0)))
        order.append((12.0, lambda ab: pass_second(ab, 1)))
        order.append((15.0, lambda ab: share(ab, 3)))
        order.append((15.0, lambda ab: pass_second(ab, 2)))
        order.append((16.0, lambda ab: share(ab, 1)))
        order.append((19.0, lambda ab: share(ab, 2)))
        for j in range(4):
            order.append((100.0, lambda ab, j=j: finish(ab, j)))
        for at, step in order:
            for ab in range(2):
                events.append((start + at, functools.partial(step, ab)))

    for copy in local:
        copy.wait()
    plane(0, zh, 0.0)
    plane(1, 1 - zh, 20.0)
    for _, step in sorted(events, key=lambda e: e[0]):
        step()
    for copy, when in sent:
        if when is None:
            copy.wait_send()
        else:
            pl.when(when)(copy.wait_send)


def gather(blocks):
    return pl.pallas_call(
        gather_kernel,
        out_shape=(
            jax.ShapeDtypeStruct((NZL, 2, HALF, 128), jnp.float32),
            jax.ShapeDtypeStruct((2, NZH, NK, 4, 4, HALF, 128), jnp.float32),
        ),
        in_specs=[pl.BlockSpec(memory_space=pltpu.VMEM)],
        out_specs=(pl.BlockSpec(memory_space=pltpu.HBM), pl.BlockSpec(memory_space=pltpu.HBM)),
        scratch_shapes=[
            pltpu.VMEM((2, HALF, 128), jnp.float32),
            pltpu.SemaphoreType.DMA((3,)),
            pltpu.SemaphoreType.DMA((2, 2, NZL - 1, 2)),
            pltpu.SemaphoreType.DMA((2, 2)),
            pltpu.SemaphoreType.DMA((2, 2, 2, 20)),
            pltpu.SemaphoreType.DMA((2, 2, 2, 4)),
        ],
        compiler_params=pltpu.CompilerParams(collective_id=0, has_side_effects=True, vmem_limit_bytes=16 << 20),
        name="gather_rows_and_columns",
    )(blocks)


def product_kernel(table, left_ref, right_ref, out_ref, part_ref, held, codes, sem):
    me = here()
    c = me["zl"]
    row = lax.axis_index("row")
    first = row * WIDTH + lax.axis_index("layer") * 2
    out_ref[...] = jnp.zeros_like(out_ref)

    def fetch(n, code):
        m = code // 16
        u = code // 4 % 4
        group, inner = m // WIDTH, m % WIDTH
        ab, ky, kk = inner % 2, inner // 4, inner // 2 % 2
        gx = group % NX
        p = jnp.where(ab == 0, gx, ky)
        q = jnp.where(ab == 0, ky, gx)
        return pltpu.make_async_copy(
            right_ref.at[ab, group // NX, kk, p, q, pl.ds(pl.multiple_of(u * PACK, 8), PACK)], held.at[n], sem.at[n])

    def find(e, n):
        i, slot = e // (GROUPS * SLOTS), e % (GROUPS * SLOTS)
        at = first + i
        base = at * (GROUPS * SLOTS)
        col = table[base + slot]
        m = slot // SLOTS * WIDTH + col

        def inner(n):
            for u in range(SLOTS):
                j = table[m * (GROUPS * SLOTS) + c * SLOTS + u]
                s = jnp.int32(3)
                for t in range(SLOTS):
                    s = jnp.where(j == table[base + c * SLOTS + t], t, s)
                hit = jnp.logical_and(j >= 0, s < 3)
                code = (m * 4 + u) * 4 + s

                @pl.when(hit)
                def _():
                    codes[2 * n] = code
                    codes[2 * n + 1] = e
                    fetch(n, code).start()

                n = n + hit.astype(jnp.int32)
            return n

        return lax.cond(col >= 0, inner, lambda n: n, n)

    count = lax.fori_loop(0, 2 * GROUPS * SLOTS, find, jnp.int32(0))

    def multiply(n, _):
        code, e = codes[2 * n], codes[2 * n + 1]
        i, slot = e // (GROUPS * SLOTS), e % (GROUPS * SLOTS)
        fetch(n, code).wait()
        start = pl.multiple_of(slot % SLOTS * PACK, 8)
        a = unpack(left_ref[slot // SLOTS, i, pl.ds(start, PACK), :])
        b = unpack(held[n])
        a_hi, b_hi = a.astype(jnp.bfloat16), b.astype(jnp.bfloat16)
        a_lo = (a - a_hi.astype(jnp.float32)).astype(jnp.bfloat16)
        b_lo = (b - b_hi.astype(jnp.float32)).astype(jnp.bfloat16)
        dot = functools.partial(jnp.dot, preferred_element_type=jnp.float32)
        out_ref[i, 0, code % 4] += dot(a_hi, b_hi) + (dot(a_lo, b_hi) + dot(a_hi, b_lo))
        return 0

    lax.fori_loop(0, count, multiply, 0)

    part_ref[...] = jnp.zeros_like(part_ref)

    @pl.when(row == c)
    def _():
        total = jnp.float32(0)
        eye = lax.broadcasted_iota(jnp.int32, (B, B), 0) == lax.broadcasted_iota(jnp.int32, (B, B), 1)
        for i in range(2):
            for s in range(SLOTS):
                on = table[(first + i) * (GROUPS * SLOTS) + c * SLOTS + s] == (first + i) % WIDTH
                total += jnp.sum(jnp.where(jnp.logical_and(eye, on), out_ref[i, 0, s], 0.0))
        part_ref[...] = jnp.full(part_ref.shape, total, jnp.float32)


def local_product(table, left, right):
    return pl.pallas_call(
        product_kernel,
        out_shape=(
            jax.ShapeDtypeStruct((2, 1, SLOTS, B, B), jnp.float32),
            jax.ShapeDtypeStruct((8, 128), jnp.float32),
        ),
        in_specs=[
            pl.BlockSpec(memory_space=pltpu.SMEM),
            pl.BlockSpec(memory_space=pltpu.VMEM),
            pl.BlockSpec(memory_space=pltpu.HBM),
        ],
        out_specs=(pl.BlockSpec(memory_space=pltpu.VMEM), pl.BlockSpec(memory_space=pltpu.VMEM)),
        scratch_shapes=[
            pltpu.VMEM((MAXHIT, PACK, 128), jnp.float32),
            pltpu.SMEM((2 * MAXHIT,), jnp.int32),
            pltpu.SemaphoreType.DMA((MAXHIT,)),
        ],
        compiler_params=pltpu.CompilerParams(vmem_limit_bytes=24 << 20),
        name="matched_products",
    )(table, left, right)


def total_kernel(v_ref, o_ref, in_plane, along, one, psem, zsem):
    me = here()
    z = me["zh"] * NZL + me["zl"]
    mine = (me["x"] * NY + me["y"]) * NK + me["k"]
    n_plane, n_z = NX * NY * NK, NZH * NZL
    barrier = pltpu.get_barrier_semaphore()

    def in_plane_at(j):
        t = (mine + j) % n_plane
        return {"x": t // (NY * NK), "y": t // NK % NY, "k": t % NK, "zh": me["zh"], "zl": me["zl"]}

    for j in range(1, n_plane):
        pl.semaphore_signal(barrier, inc=1, device_id=device(in_plane_at(j)), device_id_type=MESH)
    for j in range(1, n_z):
        pl.semaphore_signal(barrier, inc=1, device_id=device(moved(me, "z", j)), device_id_type=MESH)
    in_plane[mine] = v_ref[...]
    pl.semaphore_wait(barrier, n_plane + n_z - 2)
    copies = []
    for j in range(1, n_plane):
        copy = pltpu.make_async_remote_copy(
            src_ref=in_plane.at[mine], dst_ref=in_plane.at[mine], send_sem=psem.at[0, j], recv_sem=psem.at[1, j],
            device_id=device(in_plane_at(j)), device_id_type=MESH)
        copy.start()
        copies.append(copy)
    for copy in copies:
        copy.wait_recv()
    one[...] = jnp.sum(in_plane[...], axis=0)
    along[z] = one[...]
    more = []
    for j in range(1, n_z):
        copy = pltpu.make_async_remote_copy(
            src_ref=one, dst_ref=along.at[z], send_sem=zsem.at[0, j], recv_sem=zsem.at[1, j],
            device_id=device(moved(me, "z", j)), device_id_type=MESH)
        copy.start()
        more.append(copy)
    for copy in more:
        copy.wait_recv()
    o_ref[...] = jnp.sum(along[...], axis=0)
    for copy in copies + more:
        copy.wait_send()


def total(part):
    return pl.pallas_call(
        total_kernel,
        out_shape=jax.ShapeDtypeStruct((8, 128), jnp.float32),
        in_specs=[pl.BlockSpec(memory_space=pltpu.VMEM)],
        out_specs=pl.BlockSpec(memory_space=pltpu.VMEM),
        scratch_shapes=[
            pltpu.VMEM((NX * NY * NK, 8, 128), jnp.float32),
            pltpu.VMEM((NZH * NZL, 8, 128), jnp.float32),
            pltpu.VMEM((8, 128), jnp.float32),
            pltpu.SemaphoreType.DMA((2, NX * NY * NK)),
            pltpu.SemaphoreType.DMA((2, NZH * NZL)),
        ],
        compiler_params=pltpu.CompilerParams(collective_id=1, has_side_effects=True),
        name="trace_total",
    )(part)


def body(blocks, block_cols, occupancy):
    table = jnp.where(occupancy == 1, block_cols, -1).reshape(-1)
    left, right = gather(blocks)
    product, part = local_product(table, left, right)
    return product, total(part)[0, 0]


def solution(mesh):
    in_specs = (P(("row", "layer"), "col", None, None, None), P(), P())
    out_specs = (P(("row", "layer"), "col", None, None, None), P())
    return jax.shard_map(body, mesh=mesh, in_specs=in_specs, out_specs=out_specs, check_vma=False)
```

```python
import functools

import jax
import jax.numpy as jnp
from jax import lax
from jax.experimental import pallas as pl
from jax.experimental.pallas import tpu as pltpu
from jax.sharding import PartitionSpec as P

MESH = pl.DeviceIdType.MESH
NX, NY, NZH, NZL, NK = 4, 4, 2, 8, 2
NZ = NZH * NZL
B, SLOTS, PACK = 96, 3, 72
CUT = 32
NB, GROUPS, WIDTH = 128, 8, 16
ROW = GROUPS * SLOTS
QUAD = GROUPS // NZH
DEPTH = QUAD * SLOTS * 128

T_RING, T_TAIL0, T_TAIL, T_FAR = 2.7, 12.0, 3.0, 21.6
AT_NEAR, AT_LEFT = 29.6, 36.0


def here():
    r, c, l = lax.axis_index("row"), lax.axis_index("col"), lax.axis_index("layer")
    return {"x": r % NX, "zh": r // NX, "zl": c, "y": l // NK, "k": l % NK}


def device(at):
    return {"row": at["zh"] * NX + at["x"], "col": at["zl"], "layer": at["y"] * NK + at["k"]}


def moved(at, axis, by):
    at = dict(at)
    if axis == "x":
        at["x"] = (at["x"] + by + NX) % NX
    elif axis == "y":
        at["y"] = (at["y"] + by + NY) % NY
    elif axis == "k":
        at["k"] = 1 - at["k"]
    else:
        z = (at["zh"] * NZL + at["zl"] + by + NZ) % NZ
        at["zh"], at["zl"] = z // NZL, z % NZL
    return at


def pack(block):
    rest = block[PACK:, :]
    side = jnp.concatenate([rest[:, 0:32], rest[:, 32:64], rest[:, 64:96]], axis=0)
    return jnp.concatenate([block[:PACK, :], side], axis=1)


def unpack(packed):
    side = packed[:, B:]
    rest = jnp.concatenate([side[0:24], side[24:48], side[48:72]], axis=1)
    return jnp.concatenate([packed[:, :B], rest], axis=0)


def split(value):
    high = value.astype(jnp.bfloat16)
    return high, (value - high.astype(jnp.float32)).astype(jnp.bfloat16)


def kernel(table, b_ref, out_ref, trace_ref, raw, own, line, near, far, lhs, rhs_hi, rhs_lo, in_plane, along, one, two,
           lsem, s1sem, s2sem, xsem, dsem, psem, zsem):
    me = here()
    zl, zh, x, y, k = me["zl"], me["zh"], me["x"], me["y"], me["k"]
    z = zh * NZL + zl
    partners = [moved(me, *step) for step in (
        ("z", 1), ("z", -1), ("x", 1), ("x", -1), ("x", 2), ("y", 1), ("y", -1), ("y", 2), ("k", 1))]
    barrier = pltpu.get_barrier_semaphore()
    for other in partners:
        pl.semaphore_signal(barrier, inc=1, device_id=device(other), device_id_type=MESH)
    load = pltpu.make_async_copy(b_ref, raw, lsem.at[0])
    load.start()
    load.wait()
    for i in range(2):
        for s in range(SLOTS):
            own[i, s] = pack(raw[i, 0, s])
    local = [
        pltpu.make_async_copy(own, line.at[z], lsem.at[0]),
        pltpu.make_async_copy(own.at[0], near.at[0, k, x, y], lsem.at[1]),
        pltpu.make_async_copy(own.at[1], near.at[1, k, x, y], lsem.at[2]),
    ]
    for copy in local:
        copy.start()
    pl.semaphore_wait(barrier, len(partners))

    sent = []

    def send(src, dst, to, sems, index, when=None):
        copy = pltpu.make_async_remote_copy(
            src_ref=src, dst_ref=dst, send_sem=sems.at[(0,) + index], recv_sem=sems.at[(1,) + index],
            device_id=device(to), device_id_type=MESH)
        if when is None:
            copy.start()
        else:
            pl.when(when)(copy.start)
        sent.append((copy, when))
        return copy

    events = []

    ring, tail = {}, {}

    def ring_step(d, n, c):
        way = 1 - 2 * d
        origin = (z - way * n + NZ) % NZ
        if n > 0:
            ring[d, n - 1, c].wait_recv()
        if n < NZL:
            src = own.at[d, c] if n == 0 else line.at[origin, d, c]
            dst = line.at[origin, d, c] if n < NZL - 1 else far.at[d, k, x, y, c]
            ring[d, n, c] = send(src, dst, moved(me, "z", way), s1sem, (d, n, c))

    def tail_step(d, n, c):
        way = 1 - 2 * d
        part = 1 - d
        piece = jnp.clip(zl - way * n, 0, NZL - 1)
        origin = zh * NZL + piece
        got = (zl >= n) if d == 0 else (zl + n < NZL)
        more = (zl < NZL - 1) if d == 0 else (zl > 0)
        if n > 0:
            pl.when(got)(tail[d, n - 1, c].wait_recv)
        if n < NZL - 1:
            src = own.at[part, c] if n == 0 else line.at[origin, part, c]
            tail[d, n, c] = send(src, line.at[origin, part, c], moved(me, "z", way), s2sem, (d, n, c),
                                 jnp.logical_and(got, more))

    for n in range(NZL):
        for c in range(SLOTS):
            for d in range(2):
                events.append((T_RING * n + 0.76 * c, functools.partial(ring_step, d, n, c)))
                events.append((2.3 if n == 0 else T_TAIL0 + T_TAIL * n + 0.76 * c, functools.partial(tail_step, d, n, c)))

    def plane(phase, store, start):
        first, second = ("x", "y"), ("y", "x")
        size = {"x": NX, "y": NY}
        chunks = {}

        def ref(ab, p, q, d=None):
            view = store.at[ab, k, p, q] if ab == 0 else store.at[ab, k, q, p]
            if d is None:
                return view
            low = CUT if ab == 0 else PACK - CUT
            return view.at[:, pl.ds(0, low)] if d == 0 else view.at[:, pl.ds(low, PACK - low)]

        def spot(axis, by):
            return (me[axis] + by + size[axis]) % size[axis]

        def go(ab, p, q, axis, way, sem, d=None):
            r = ref(ab, p, q, d)
            return send(r, r, moved(me, axis, way), xsem, (phase, ab, sem))

        def spread(ab, j):
            a, b = first[ab], second[ab]
            for d, way in enumerate((1, -1)):
                chunks[ab, "b", j, d] = go(ab, spot(a, j), me[b], b, way, 3 + 4 * j + d)

        def begin(ab):
            a = first[ab]
            if phase == 1:
                for c in range(SLOTS):
                    ring_step(ab, NZL, c)
            for d, way in enumerate((1, -1, 2)):
                chunks[ab, "a", d] = go(ab, me[a], me[second[ab]], a, way, d)

        def pass_on(ab, d):
            chunks[ab, "a", d].wait_recv()
            spread(ab, (3, 1, 2)[d])

        def pass_second(ab, j):
            a, b = first[ab], second[ab]
            for d, way in enumerate((1, -1)):
                chunks[ab, "b", j, d].wait_recv()
                chunks[ab, "b2", j, d] = go(ab, spot(a, j), spot(b, -way), b, way, 5 + 4 * j + d, d)

        def share(ab, j):
            for d in range(2):
                chunks[ab, "b2", j, d].wait_recv()
            p = spot(first[ab], j)
            src = store.at[ab, k, p] if ab == 0 else store.at[ab, k, :, p]
            chunks[ab, "c", j] = send(src, src, moved(me, "k", 1), dsem, (phase, ab, j))

        def finish(ab, j):
            chunks[ab, "c", j].wait_recv()

        order = [
            (0.0, begin), (0.01, lambda ab: spread(ab, 0)),
            (4.5, lambda ab: pass_on(ab, 0)), (4.5, lambda ab: pass_on(ab, 1)),
            (9.0, lambda ab: pass_on(ab, 2)), (9.1, lambda ab: pass_second(ab, 0)),
            (12.5, lambda ab: pass_second(ab, 3)), (14.7, lambda ab: pass_second(ab, 1)),
            (15.8, lambda ab: share(ab, 0)), (18.1, lambda ab: share(ab, 3)),
            (18.2, lambda ab: pass_second(ab, 2)), (20.4, lambda ab: share(ab, 1)), (22.6, lambda ab: share(ab, 2)),
        ]
        for j in range(4):
            order.append((24.0 if phase == 0 else 1000.0, lambda ab, j=j: finish(ab, j)))
        for at, step in order:
            for ab in range(2):
                events.append((start + at, functools.partial(step, ab)))

    for copy in local:
        copy.wait()
    plane(0, near, 0.0)
    plane(1, far, T_FAR)

    first_row = lax.axis_index("row") * WIDTH + lax.axis_index("layer") * 2

    def left_side(i, half, h, g4):
        for t in range(SLOTS):
            high, low = split(unpack(line[zh * NZL + h * QUAD + g4, i, t]))
            lanes = pl.ds(pl.multiple_of((g4 * SLOTS + t) * 128, 128), B)
            lhs[i, half, 0:B, lanes] = high
            lhs[i, half, B:2 * B, lanes] = low

    def right_side(i, half, h, g4):
        store = near if half == 0 else far
        base = (first_row + i) * ROW
        group = h * QUAD + g4
        wanted = [table[base + zl * SLOTS + s] for s in range(SLOTS)]
        for t in range(SLOTS):
            col = table[base + group * SLOTS + t]
            inner = jnp.maximum(col, 0)
            at = (group * WIDTH + inner) * ROW + zl * SLOTS
            cols = [table[at + u] for u in range(SLOTS)]
            depth = pl.ds(pl.multiple_of((g4 * SLOTS + t) * 128, 128), B)
            for s in range(SLOTS):
                want = jnp.where(col >= 0, wanted[s] + 1, 0)
                hits = [jnp.where(cols[u] + 1 == want, 1, 0) * jnp.where(want > 0, 1, 0) for u in range(SLOTS)]
                u = jnp.minimum(hits[1] + 2 * hits[2], SLOTS - 1)
                on = jnp.minimum(hits[0] + hits[1] + hits[2], 1).astype(jnp.float32)
                block = store[inner & 1, (inner >> 1) & 1, g4, inner >> 2, u] * on
                high, low = split(unpack(block))
                rhs_hi[i, half, depth, s * 128:s * 128 + B] = high
                rhs_lo[i, half, depth, s * 128:s * 128 + B] = low

    def multiply(i, half):
        dot = functools.partial(jnp.dot, preferred_element_type=jnp.float32)
        main = dot(lhs[i, half], rhs_hi[i, half])
        rest = dot(lhs[i, half, 0:B, :], rhs_lo[i, half])
        value = main[0:B] + (main[B:] + rest)
        for s in range(SLOTS):
            part = value[:, s * 128:s * 128 + B]
            if half == 0:
                out_ref[i, 0, s] = part
            else:
                out_ref[i, 0, s] += part

    def clear(ref):
        ref[...] = jnp.zeros_like(ref)

    def prepare():
        for i in range(2):
            for half in range(2):
                clear(lhs.at[i, half])
                clear(rhs_hi.at[i, half])
                clear(rhs_lo.at[i, half])

    def every(fn, half, h):
        def step(n, _):
            fn(n // QUAD, half, h, n % QUAD)
            return 0
        lax.fori_loop(0, 2 * QUAD, step, 0)

    other = 1 - zh
    events.append((0.3, prepare))
    events.append((AT_NEAR, lambda: every(right_side, 0, zh)))
    events.append((AT_LEFT, lambda: every(left_side, 0, zh)))
    events.append((AT_LEFT + 1.5, lambda: every(left_side, 1, other)))
    for i in range(2):
        events.append((AT_LEFT + 2.5 + i, functools.partial(multiply, i, 0)))
    for _, step in sorted(events, key=lambda e: e[0]):
        step()
    every(right_side, 1, other)
    for i in range(2):
        multiply(i, 1)

    row, col = lax.axis_index("row"), lax.axis_index("col")
    diagonal = row == col
    n_yk = NY * NK
    def own_trace():
        eye = lax.broadcasted_iota(jnp.int32, (B, B), 0) == lax.broadcasted_iota(jnp.int32, (B, B), 1)
        total = jnp.zeros((1, B), jnp.float32)
        for i in range(2):
            for s in range(SLOTS):
                at = first_row + i
                on = table[at * ROW + zl * SLOTS + s] == at % WIDTH
                total += jnp.sum(jnp.where(eye, out_ref[i, 0, s], 0.0), axis=0, keepdims=True) * jnp.where(on, 1.0, 0.0)
        one[...] = jnp.full((8, 128), jnp.sum(total), jnp.float32)

    mine = y * NK + k

    def plane_copy(j):
        dx, t = (2, 1, 3, 0)[j // n_yk], (mine + j % n_yk) % n_yk
        to = {"x": (x + dx) % NX, "y": t // NK, "k": t % NK, "zh": zh, "zl": zl}
        return pltpu.make_async_remote_copy(
            src_ref=one, dst_ref=in_plane.at[mine], send_sem=psem.at[0, j], recv_sem=psem.at[1, j],
            device_id=device(to), device_id_type=MESH)

    n_plane = NX * n_yk
    plane_copies = [plane_copy(j) for j in range(n_plane) if j != 3 * n_yk]

    @pl.when(diagonal)
    def _():
        own_trace()
        for copy in plane_copies:
            copy.start()
        in_plane[mine] = one[...]

    holds = zh == zl // NX
    dx_in = (x - zl % NX + NX) % NX
    for slot, dx in enumerate((2, 1, 3, 0)):
        @pl.when(jnp.logical_and(holds, dx_in == dx))
        def _():
            for t in range(n_yk):
                if dx != 0 or t != 0:
                    plane_copy(slot * n_yk + t).wait_recv()

    def z_copy(j):
        return pltpu.make_async_remote_copy(
            src_ref=two, dst_ref=along.at[zl], send_sem=zsem.at[0, j], recv_sem=zsem.at[1, j],
            device_id=device(moved(me, "z", j)), device_id_type=MESH)

    z_order = sorted(range(1, NZ), key=lambda j: -min(j, NZ - j))

    @pl.when(holds)
    def _():
        two[...] = jnp.sum(in_plane[...], axis=0)
        for j in z_order:
            z_copy(j).start()
        along[zl] = two[...]

    for j in range(1, NZ):
        zs = (z - j + NZ) % NZ
        @pl.when(zs // NZL == zs % NZL // NX)
        def _():
            z_copy(j).wait_recv()
    trace_ref[...] = jnp.sum(along[...], axis=0)

    @pl.when(holds)
    def _():
        for j in z_order:
            z_copy(j).wait_send()

    @pl.when(diagonal)
    def _():
        for copy in plane_copies:
            copy.wait_send()
    for copy, when in sent:
        if when is None:
            copy.wait_send()
        else:
            pl.when(when)(copy.wait_send)


def square(table, blocks, collective_id=0, name="square"):
    return pl.pallas_call(
        kernel,
        out_shape=(jax.ShapeDtypeStruct((2, 1, SLOTS, B, B), jnp.float32), jax.ShapeDtypeStruct((8, 128), jnp.float32)),
        in_specs=[pl.BlockSpec(memory_space=pltpu.SMEM), pl.BlockSpec(memory_space=pl.ANY)],
        out_specs=(pl.BlockSpec(memory_space=pltpu.VMEM), pl.BlockSpec(memory_space=pltpu.VMEM)),
        scratch_shapes=[
            pltpu.VMEM((2, 1, SLOTS, B, B), jnp.float32),
            pltpu.VMEM((2, SLOTS, PACK, 128), jnp.float32),
            pltpu.VMEM((NZ, 2, SLOTS, PACK, 128), jnp.float32),
            pltpu.VMEM((2, NK, NX, NY, SLOTS, PACK, 128), jnp.float32),
            pltpu.VMEM((2, NK, NX, NY, SLOTS, PACK, 128), jnp.float32),
            pltpu.VMEM((2, 2, 2 * B, DEPTH), jnp.bfloat16),
            pltpu.VMEM((2, 2, DEPTH, SLOTS * 128), jnp.bfloat16),
            pltpu.VMEM((2, 2, DEPTH, SLOTS * 128), jnp.bfloat16),
            pltpu.VMEM((NY * NK, 8, 128), jnp.float32),
            pltpu.VMEM((NZL, 8, 128), jnp.float32),
            pltpu.VMEM((8, 128), jnp.float32),
            pltpu.VMEM((8, 128), jnp.float32),
            pltpu.SemaphoreType.DMA((3,)),
            pltpu.SemaphoreType.DMA((2, 2, NZL, SLOTS)),
            pltpu.SemaphoreType.DMA((2, 2, NZL, SLOTS)),
            pltpu.SemaphoreType.DMA((2, 2, 2, 20)),
            pltpu.SemaphoreType.DMA((2, 2, 2, 4)),
            pltpu.SemaphoreType.DMA((2, NX * NY * NK)),
            pltpu.SemaphoreType.DMA((2, NZ)),
        ],
        compiler_params=pltpu.CompilerParams(collective_id=collective_id, has_side_effects=True, vmem_limit_bytes=48 << 20),
        name=name,
    )(table, blocks)


def body(blocks, block_cols, occupancy):
    table = jnp.where(occupancy == 1, block_cols, -1).reshape(-1)
    product, trace = square(table, blocks)
    return product, trace[0, 0]


def solution(mesh):
    in_specs = (P(("row", "layer"), "col", None, None, None), P(), P())
    out_specs = (P(("row", "layer"), "col", None, None, None), P())
    return jax.shard_map(body, mesh=mesh, in_specs=in_specs, out_specs=out_specs, check_vma=False)
```

```python
import functools

import jax
import jax.numpy as jnp
from jax import lax
from jax.experimental import pallas as pl
from jax.experimental.pallas import tpu as pltpu
from jax.sharding import PartitionSpec as P

MESH = pl.DeviceIdType.MESH
NX, NY, NZH, NZL, NK = 4, 4, 2, 8, 2
NZ = NZH * NZL
LEAPS = NZL // 2
B, SLOTS, PACK = 96, 3, 72
CUT = 32
NB, GROUPS, WIDTH = 128, 8, 16
QUAD = GROUPS // NZH
DEPTH = QUAD * SLOTS * 128

T_RING, T_OWN, T_TAIL0, T_TAIL, T_SIDE0, T_SIDE, T_FAR = 3.6, 13.0, 14.0, 3.0, 18.0, 2.0, 16.0
AT_NEAR, AT_LEFT = 24.5, 37.0


def here():
    r, c, l = lax.axis_index("row"), lax.axis_index("col"), lax.axis_index("layer")
    return {"x": r % NX, "zh": r // NX, "zl": c, "y": l // NK, "k": l % NK}


def device(at):
    return {"row": at["zh"] * NX + at["x"], "col": at["zl"], "layer": at["y"] * NK + at["k"]}


def moved(at, axis, by):
    at = dict(at)
    if axis == "x":
        at["x"] = (at["x"] + by + NX) % NX
    elif axis == "y":
        at["y"] = (at["y"] + by + NY) % NY
    elif axis == "k":
        at["k"] = 1 - at["k"]
    else:
        z = (at["zh"] * NZL + at["zl"] + by + NZ) % NZ
        at["zh"], at["zl"] = z // NZL, z % NZL
    return at


def pack(block):
    rest = block[PACK:, :]
    side = jnp.concatenate([rest[:, 0:32], rest[:, 32:64], rest[:, 64:96]], axis=0)
    return jnp.concatenate([block[:PACK, :], side], axis=1)


def unpack(packed):
    side = packed[:, B:]
    rest = jnp.concatenate([side[0:24], side[24:48], side[48:72]], axis=1)
    return jnp.concatenate([packed[:, :B], rest], axis=0)


def split(value):
    high = value.astype(jnp.bfloat16)
    return high, (value - high.astype(jnp.float32)).astype(jnp.bfloat16)


def kernel(table, b_ref, out_ref, trace_ref, raw, own, line, near, far, lhs, rhs_hi, rhs_lo, in_plane, along, one, two,
           lsem, s1sem, s2sem, xsem, dsem, psem, zsem):
    me = here()
    zl, zh, x, y, k = me["zl"], me["zh"], me["x"], me["y"], me["k"]
    z = zh * NZL + zl
    steps = [("z", 1), ("z", -1), ("z", 2), ("z", -2), ("x", 1), ("x", -1), ("x", 2), ("y", 1), ("y", -1), ("y", 2), ("k", 1)]
    near_by = {step: moved(me, *step) for step in steps}
    ids = {step: device(at) for step, at in near_by.items()}
    spots = {(axis, by): near_by[axis, by if by < 3 else -1][axis] if by else me[axis] for axis in ("x", "y") for by in range(4)}
    ups = [(z + j) % NZ for j in range(NZ)]
    barrier = pltpu.get_barrier_semaphore()
    for step in steps:
        pl.semaphore_signal(barrier, inc=1, device_id=ids[step], device_id_type=MESH)
    load = pltpu.make_async_copy(b_ref, raw, lsem.at[0])
    load.start()
    load.wait()
    for i in range(2):
        for s in range(SLOTS):
            own[i, s] = pack(raw[i, 0, s])
    local = [
        pltpu.make_async_copy(own, line.at[z], lsem.at[0]),
        pltpu.make_async_copy(own.at[0], near.at[0, k, x, y], lsem.at[1]),
        pltpu.make_async_copy(own.at[1], near.at[1, k, x, y], lsem.at[2]),
    ]
    for copy in local:
        copy.start()
    pl.semaphore_wait(barrier, len(steps))

    sent = []

    def send(src, dst, to, sems, index, when=None):
        copy = pltpu.make_async_remote_copy(
            src_ref=src, dst_ref=dst, send_sem=sems.at[(0,) + index], recv_sem=sems.at[(1,) + index],
            device_id=ids[to], device_id_type=MESH)
        if when is None:
            copy.start()
        else:
            pl.when(when)(copy.start)
        sent.append((copy, when))
        return copy

    events = []

    ring, side, tail = {}, {}, {}

    def ring_step(d, m, c):
        way = 1 - 2 * d
        origin = ups[-way * 2 * m % NZ]
        if m > 0:
            ring[d, m - 1, c].wait_recv()
        if m < LEAPS:
            src = own.at[d, c] if m == 0 else line.at[origin, d, c]
            dst = line.at[origin, d, c] if m < LEAPS - 1 else far.at[d, k, x, y, c]
            ring[d, m, c] = send(src, dst, ("z", 2 * way), s1sem, (d, m, c))

    def side_send(d, m, c):
        way = 1 - 2 * d
        origin, to = ups[-way * 2 * m % NZ], ups[way % NZ]
        src = own.at[d, c] if m == 0 else line.at[origin, d, c]
        side[d, m, c] = send(src, line.at[origin, d, c], ("z", way), s1sem, (d, LEAPS + m, c), origin // NZL == to // NZL)

    def side_wait(d, m, c):
        way = 1 - 2 * d
        pl.when(ups[-way * (2 * m + 1) % NZ] // NZL == zh)(side[d, m, c].wait_recv)

    def tail_step(d, n, c):
        way = 1 - 2 * d
        part = 1 - d
        piece = jnp.clip(zl - way * n, 0, NZL - 1)
        origin = zh * NZL + piece
        got = (zl >= n) if d == 0 else (zl + n < NZL)
        more = (zl < NZL - 1) if d == 0 else (zl > 0)
        if n > 0:
            pl.when(got)(tail[d, n - 1, c].wait_recv)
        if n < NZL - 1:
            src = own.at[part, c] if n == 0 else line.at[origin, part, c]
            tail[d, n, c] = send(src, line.at[origin, part, c], ("z", way), s2sem, (d, n, c),
                                 jnp.logical_and(got, more))

    for c in range(SLOTS):
        for d in range(2):
            for m in range(LEAPS):
                events.append((T_RING * m + 0.76 * c, functools.partial(ring_step, d, m, c)))
                events.append((T_SIDE0 + T_SIDE * m + 0.76 * c, functools.partial(side_send, d, m, c)))
                events.append((T_SIDE0 + T_SIDE * m + 8.0 + 0.76 * c, functools.partial(side_wait, d, m, c)))
            for n in range(NZL):
                events.append((T_OWN if n == 0 else T_TAIL0 + T_TAIL * n + 0.76 * c, functools.partial(tail_step, d, n, c)))

    def plane(phase, store, start):
        first, second = ("x", "y"), ("y", "x")
        chunks = {}

        def ref(ab, p, q, d=None):
            view = store.at[ab, k, p, q] if ab == 0 else store.at[ab, k, q, p]
            if d is None:
                return view
            low = CUT if ab == 0 else PACK - CUT
            return view.at[:, pl.ds(0, low)] if d == 0 else view.at[:, pl.ds(low, PACK - low)]

        def spot(axis, by):
            return spots[axis, by % 4]

        def go(ab, p, q, axis, way, sem, d=None):
            r = ref(ab, p, q, d)
            return send(r, r, (axis, way), xsem, (phase, ab, sem))

        def spread(ab, j):
            a, b = first[ab], second[ab]
            for d, way in enumerate((1, -1)):
                chunks[ab, "b", j, d] = go(ab, spot(a, j), me[b], b, way, 3 + 4 * j + d)

        def begin(ab):
            a = first[ab]
            if phase == 1:
                for c in range(SLOTS):
                    ring_step(ab, LEAPS, c)
            for d, way in enumerate((1, -1, 2)):
                chunks[ab, "a", d] = go(ab, me[a], me[second[ab]], a, way, d)

        def pass_on(ab, d):
            chunks[ab, "a", d].wait_recv()
            spread(ab, (3, 1, 2)[d])

        def pass_second(ab, j):
            a, b = first[ab], second[ab]
            for d, way in enumerate((1, -1)):
                chunks[ab, "b", j, d].wait_recv()
                chunks[ab, "b2", j, d] = go(ab, spot(a, j), spot(b, -way), b, way, 5 + 4 * j + d, d)

        def share(ab, j):
            for d in range(2):
                chunks[ab, "b2", j, d].wait_recv()
            p = spot(first[ab], j)
            src = store.at[ab, k, p] if ab == 0 else store.at[ab, k, :, p]
            chunks[ab, "c", j] = send(src, src, ("k", 1), dsem, (phase, ab, j))

        def finish(ab, j):
            chunks[ab, "c", j].wait_recv()

        order = [
            (0.0, begin), (0.01, lambda ab: spread(ab, 0)),
            (4.5, lambda ab: pass_on(ab, 0)), (4.5, lambda ab: pass_on(ab, 1)),
            (9.0, lambda ab: pass_on(ab, 2)), (9.1, lambda ab: pass_second(ab, 0)),
            (12.5, lambda ab: pass_second(ab, 3)), (14.7, lambda ab: pass_second(ab, 1)),
            (15.8, lambda ab: share(ab, 0)), (18.1, lambda ab: share(ab, 3)),
            (18.2, lambda ab: pass_second(ab, 2)), (20.4, lambda ab: share(ab, 1)), (22.6, lambda ab: share(ab, 2)),
        ]
        for j in range(4):
            order.append((24.0 if phase == 0 else 1000.0, lambda ab, j=j: finish(ab, j)))
        for at, step in order:
            for ab in range(2):
                events.append((start + at, functools.partial(step, ab)))

    for copy in local:
        copy.wait()
    plane(0, near, 0.0)
    plane(1, far, T_FAR)

    first_row = lax.axis_index("row") * WIDTH + lax.axis_index("layer") * 2

    def held(block_row, group, slot):
        return table[(slot * GROUPS + group) * NB + block_row]

    def left_side(i, half, h, g4):
        free = jnp.zeros((B, 128 - B), jnp.bfloat16)
        for t in range(SLOTS):
            high, low = split(unpack(line[zh * NZL + h * QUAD + g4, i, t]))
            lanes = pl.ds(pl.multiple_of((g4 * SLOTS + t) * 128, 128), 128)
            lhs[i, half, 0:B, lanes] = jnp.concatenate([high, free], axis=1)
            lhs[i, half, B:2 * B, lanes] = jnp.concatenate([low, free], axis=1)

    def right_side(slots, i, half, h, g4):
        store = near if half == 0 else far
        block_row = first_row + i
        group = h * QUAD + g4
        wanted = {s: held(block_row, zl, s) for s in slots}
        for t in range(SLOTS):
            col = held(block_row, group, t)
            inner = jnp.maximum(col, 0)
            cols = [held(group * WIDTH + inner, zl, u) for u in range(SLOTS)]
            depth = pl.ds(pl.multiple_of((g4 * SLOTS + t) * 128, 128), B)
            for s in slots:
                want = jnp.where(col >= 0, wanted[s] + 1, 0)
                hits = [jnp.where(cols[u] + 1 == want, 1, 0) * jnp.where(want > 0, 1, 0) for u in range(SLOTS)]
                u = jnp.minimum(hits[1] + 2 * hits[2], SLOTS - 1)
                on = jnp.minimum(hits[0] + hits[1] + hits[2], 1).astype(jnp.float32)
                block = store[inner & 1, (inner >> 1) & 1, g4, inner >> 2, u] * on
                high, low = split(unpack(block))
                rhs_hi[i, half, depth, s * 128:s * 128 + B] = high
                rhs_lo[i, half, depth, s * 128:s * 128 + B] = low

    def multiply(slots, i, half):
        dot = functools.partial(jnp.dot, preferred_element_type=jnp.float32)
        lanes = slice(slots[0] * 128, (slots[-1] + 1) * 128)
        main = dot(lhs[i, half], rhs_hi[i, half, :, lanes])
        rest = dot(lhs[i, half, 0:B, :], rhs_lo[i, half, :, lanes])
        value = main[0:B] + (main[B:] + rest)
        for n, s in enumerate(slots):
            part = value[:, n * 128:n * 128 + B]
            if half == 0:
                out_ref[i, 0, s] = part
            else:
                out_ref[i, 0, s] += part

    def prepare():
        for ref in (rhs_hi, rhs_lo):
            for i in range(2):
                for half in range(2):
                    for n in range(QUAD * SLOTS):
                        ref[i, half, n * 128 + B:(n + 1) * 128, :] = jnp.zeros((128 - B, SLOTS * 128), jnp.bfloat16)

    def every(fn, half, h):
        def step(n, _):
            fn(n // QUAD, half, h, n % QUAD)
            return 0
        lax.fori_loop(0, 2 * QUAD, step, 0)

    other = 1 - zh
    first, rest, whole = (0,), (1, 2), (0, 1, 2)
    events.append((0.3, prepare))
    events.append((AT_NEAR, lambda: every(functools.partial(right_side, whole), 0, zh)))
    events.append((AT_LEFT, lambda: every(left_side, 0, zh)))
    events.append((AT_LEFT + 0.5, lambda: every(left_side, 1, other)))
    for i in range(2):
        events.append((AT_LEFT + 1.0 + i, functools.partial(multiply, whole, i, 0)))
    for _, step in sorted(events, key=lambda e: e[0]):
        step()

    def far_products(slots):
        every(functools.partial(right_side, slots), 1, other)
        for i in range(2):
            multiply(slots, i, 1)

    far_products(first)
    diagonal = lax.axis_index("row") == lax.axis_index("col")
    n_yk = NY * NK
    mine = y * NK + k

    def plane_copy(j):
        dx, t = (2, 1, 3, 0)[j // n_yk], (mine + j % n_yk) % n_yk
        to = {"x": (x + dx) % NX, "y": t // NK, "k": t % NK, "zh": zh, "zl": zl}
        return pltpu.make_async_remote_copy(
            src_ref=one, dst_ref=in_plane.at[mine], send_sem=psem.at[0, j], recv_sem=psem.at[1, j],
            device_id=device(to), device_id_type=MESH)

    plane_copies = [plane_copy(j) for j in range(NX * n_yk) if j != 3 * n_yk]

    @pl.when(diagonal)
    def _():
        eye = lax.broadcasted_iota(jnp.int32, (B, B), 0) == lax.broadcasted_iota(jnp.int32, (B, B), 1)
        total = jnp.sum(jnp.where(eye, out_ref[0, 0, 0] + out_ref[1, 0, 0], 0.0))
        one[...] = jnp.full((8, 128), total, jnp.float32)
        for copy in plane_copies:
            copy.start()
        in_plane[mine] = one[...]

    far_products(rest)

    holds = zh == zl // NX
    dx_in = (x - zl % NX + NX) % NX
    for n, dx in enumerate((2, 1, 3, 0)):
        @pl.when(jnp.logical_and(holds, dx_in == dx))
        def _():
            for t in range(n_yk):
                if dx != 0 or t != 0:
                    plane_copies[n * n_yk + t - (dx == 0)].wait_recv()

    z_copies = {j: pltpu.make_async_remote_copy(
        src_ref=two, dst_ref=along.at[zl], send_sem=zsem.at[0, j], recv_sem=zsem.at[1, j],
        device_id=device(moved(me, "z", j)), device_id_type=MESH)
        for j in sorted(range(1, NZ), key=lambda j: -min(j, NZ - j))}

    @pl.when(holds)
    def _():
        two[...] = jnp.sum(in_plane[...], axis=0)
        for copy in z_copies.values():
            copy.start()
        along[zl] = two[...]

    for j, copy in z_copies.items():
        from_z = ups[-j % NZ]
        pl.when(from_z // NZL == from_z % NZL // NX)(copy.wait_recv)
    trace_ref[0, 0] = jnp.sum(along[:, 0:1, 0:1])

    @pl.when(holds)
    def _():
        for copy in z_copies.values():
            copy.wait_send()

    @pl.when(diagonal)
    def _():
        for copy in plane_copies:
            copy.wait_send()

    for copy, when in sent:
        if when is None:
            copy.wait_send()
        else:
            pl.when(when)(copy.wait_send)


def square(table, blocks, collective_id=0, name="square"):
    return pl.pallas_call(
        kernel,
        out_shape=(jax.ShapeDtypeStruct((2, 1, SLOTS, B, B), jnp.float32), jax.ShapeDtypeStruct((1, 1), jnp.float32)),
        in_specs=[pl.BlockSpec(memory_space=pltpu.SMEM), pl.BlockSpec(memory_space=pl.ANY)],
        out_specs=(pl.BlockSpec(memory_space=pltpu.VMEM), pl.BlockSpec(memory_space=pltpu.SMEM)),
        scratch_shapes=[
            pltpu.VMEM((2, 1, SLOTS, B, B), jnp.float32),
            pltpu.VMEM((2, SLOTS, PACK, 128), jnp.float32),
            pltpu.VMEM((NZ, 2, SLOTS, PACK, 128), jnp.float32),
            pltpu.VMEM((2, NK, NX, NY, SLOTS, PACK, 128), jnp.float32),
            pltpu.VMEM((2, NK, NX, NY, SLOTS, PACK, 128), jnp.float32),
            pltpu.VMEM((2, 2, 2 * B, DEPTH), jnp.bfloat16),
            pltpu.VMEM((2, 2, DEPTH, SLOTS * 128), jnp.bfloat16),
            pltpu.VMEM((2, 2, DEPTH, SLOTS * 128), jnp.bfloat16),
            pltpu.VMEM((NY * NK, 8, 128), jnp.float32),
            pltpu.VMEM((NZL, 8, 128), jnp.float32),
            pltpu.VMEM((8, 128), jnp.float32),
            pltpu.VMEM((8, 128), jnp.float32),
            pltpu.SemaphoreType.DMA((3,)),
            pltpu.SemaphoreType.DMA((2, 2, NZL, SLOTS)),
            pltpu.SemaphoreType.DMA((2, 2, NZL, SLOTS)),
            pltpu.SemaphoreType.DMA((2, 2, 2, 20)),
            pltpu.SemaphoreType.DMA((2, 2, 2, 4)),
            pltpu.SemaphoreType.DMA((2, NX * NY * NK)),
            pltpu.SemaphoreType.DMA((2, NZ)),
        ],
        compiler_params=pltpu.CompilerParams(collective_id=collective_id, has_side_effects=True, vmem_limit_bytes=48 << 20),
        name=name,
    )(table, blocks)


def body(blocks, block_cols, occupancy):
    table = jnp.where(occupancy == 1, block_cols, -1).transpose(2, 1, 0).reshape(-1)
    product, trace = square(table, blocks)
    return product, trace[0, 0]


def solution(mesh):
    in_specs = (P(("row", "layer"), "col", None, None, None), P(), P())
    out_specs = (P(("row", "layer"), "col", None, None, None), P())
    return jax.shard_map(body, mesh=mesh, in_specs=in_specs, out_specs=out_specs, check_vma=False)
```

```python
import functools

import jax
import jax.numpy as jnp
from jax import lax
from jax.experimental import pallas as pl
from jax.experimental.pallas import tpu as pltpu
from jax.sharding import PartitionSpec as P

MESH = pl.DeviceIdType.MESH
NX, NY, NZH, NZL, NK = 4, 4, 2, 8, 2
NZ = NZH * NZL
LEAPS = NZL // 2
B, SLOTS, PACK = 96, 3, 72
CUT = 32
NB, GROUPS, WIDTH = 128, 8, 16
QUAD = GROUPS // NZH
DEPTH = QUAD * SLOTS * 128

T_RING, T_OWN, T_TAIL0, T_TAIL, T_SIDE0, T_SIDE, T_FAR = 3.6, 13.0, 14.0, 3.0, 18.0, 2.0, 16.0
AT_NEAR, AT_TRACE, AT_LEFT = 24.5, 30.0, 37.0


def here():
    r, c, l = lax.axis_index("row"), lax.axis_index("col"), lax.axis_index("layer")
    return {"x": r % NX, "zh": r // NX, "zl": c, "y": l // NK, "k": l % NK}


def device(at):
    return {"row": at["zh"] * NX + at["x"], "col": at["zl"], "layer": at["y"] * NK + at["k"]}


def moved(at, axis, by):
    at = dict(at)
    if axis == "x":
        at["x"] = (at["x"] + by + NX) % NX
    elif axis == "y":
        at["y"] = (at["y"] + by + NY) % NY
    elif axis == "k":
        at["k"] = 1 - at["k"]
    else:
        z = (at["zh"] * NZL + at["zl"] + by + NZ) % NZ
        at["zh"], at["zl"] = z // NZL, z % NZL
    return at


def pack(block):
    rest = block[PACK:, :]
    side = jnp.concatenate([rest[:, 0:32], rest[:, 32:64], rest[:, 64:96]], axis=0)
    return jnp.concatenate([block[:PACK, :], side], axis=1)


def unpack(packed):
    side = packed[:, B:]
    rest = jnp.concatenate([side[0:24], side[24:48], side[48:72]], axis=1)
    return jnp.concatenate([packed[:, :B], rest], axis=0)


def split(value):
    high = value.astype(jnp.bfloat16)
    return high, (value - high.astype(jnp.float32)).astype(jnp.bfloat16)


def kernel(table, b_ref, out_ref, trace_ref, raw, own, line, near, far, lhs, rhs_hi, rhs_lo, in_plane, along, one, two, near_sum,
           lsem, s1sem, s2sem, xsem, dsem, psem, zsem):
    me = here()
    zl, zh, x, y, k = me["zl"], me["zh"], me["x"], me["y"], me["k"]
    z = zh * NZL + zl
    steps = [("z", 1), ("z", -1), ("z", 2), ("z", -2), ("x", 1), ("x", -1), ("x", 2), ("y", 1), ("y", -1), ("y", 2), ("k", 1)]
    near_by = {step: moved(me, *step) for step in steps}
    ids = {step: device(at) for step, at in near_by.items()}
    spots = {(axis, by): near_by[axis, by if by < 3 else -1][axis] if by else me[axis] for axis in ("x", "y") for by in range(4)}
    ups = [(z + j) % NZ for j in range(NZ)]
    barrier = pltpu.get_barrier_semaphore()
    for step in steps:
        pl.semaphore_signal(barrier, inc=1, device_id=ids[step], device_id_type=MESH)
    load = pltpu.make_async_copy(b_ref, raw, lsem.at[0])
    load.start()
    load.wait()
    for i in range(2):
        for s in range(SLOTS):
            own[i, s] = pack(raw[i, 0, s])
    local = [
        pltpu.make_async_copy(own, line.at[z], lsem.at[0]),
        pltpu.make_async_copy(own.at[0], near.at[0, k, x, y], lsem.at[1]),
        pltpu.make_async_copy(own.at[1], near.at[1, k, x, y], lsem.at[2]),
    ]
    for copy in local:
        copy.start()
    pl.semaphore_wait(barrier, len(steps))

    sent = []

    def send(src, dst, to, sems, index, when=None):
        copy = pltpu.make_async_remote_copy(
            src_ref=src, dst_ref=dst, send_sem=sems.at[(0,) + index], recv_sem=sems.at[(1,) + index],
            device_id=ids[to], device_id_type=MESH)
        if when is None:
            copy.start()
        else:
            pl.when(when)(copy.start)
        sent.append((copy, when))
        return copy

    events = []

    ring, side, tail = {}, {}, {}

    def ring_step(d, m, c):
        way = 1 - 2 * d
        origin = ups[-way * 2 * m % NZ]
        if m > 0:
            ring[d, m - 1, c].wait_recv()
        if m < LEAPS:
            src = own.at[d, c] if m == 0 else line.at[origin, d, c]
            dst = line.at[origin, d, c] if m < LEAPS - 1 else far.at[d, k, x, y, c]
            ring[d, m, c] = send(src, dst, ("z", 2 * way), s1sem, (d, m, c))

    def side_send(d, m, c):
        way = 1 - 2 * d
        origin, to = ups[-way * 2 * m % NZ], ups[way % NZ]
        src = own.at[d, c] if m == 0 else line.at[origin, d, c]
        side[d, m, c] = send(src, line.at[origin, d, c], ("z", way), s1sem, (d, LEAPS + m, c), origin // NZL == to // NZL)

    def side_wait(d, m, c):
        way = 1 - 2 * d
        pl.when(ups[-way * (2 * m + 1) % NZ] // NZL == zh)(side[d, m, c].wait_recv)

    def tail_step(d, n, c):
        way = 1 - 2 * d
        part = 1 - d
        piece = jnp.clip(zl - way * n, 0, NZL - 1)
        origin = zh * NZL + piece
        got = (zl >= n) if d == 0 else (zl + n < NZL)
        more = (zl < NZL - 1) if d == 0 else (zl > 0)
        if n > 0:
            pl.when(got)(tail[d, n - 1, c].wait_recv)
        if n < NZL - 1:
            src = own.at[part, c] if n == 0 else line.at[origin, part, c]
            tail[d, n, c] = send(src, line.at[origin, part, c], ("z", way), s2sem, (d, n, c),
                                 jnp.logical_and(got, more))

    for c in range(SLOTS):
        for d in range(2):
            for m in range(LEAPS):
                events.append((T_RING * m + 0.76 * c, functools.partial(ring_step, d, m, c)))
                events.append((T_SIDE0 + T_SIDE * m + 0.76 * c, functools.partial(side_send, d, m, c)))
                events.append((T_SIDE0 + T_SIDE * m + 8.0 + 0.76 * c, functools.partial(side_wait, d, m, c)))
            for n in range(NZL):
                events.append((T_OWN if n == 0 else T_TAIL0 + T_TAIL * n + 0.76 * c, functools.partial(tail_step, d, n, c)))

    def plane(phase, store, start):
        first, second = ("x", "y"), ("y", "x")
        chunks = {}

        def ref(ab, p, q, d=None):
            view = store.at[ab, k, p, q] if ab == 0 else store.at[ab, k, q, p]
            if d is None:
                return view
            low = CUT if ab == 0 else PACK - CUT
            return view.at[:, pl.ds(0, low)] if d == 0 else view.at[:, pl.ds(low, PACK - low)]

        def spot(axis, by):
            return spots[axis, by % 4]

        def go(ab, p, q, axis, way, sem, d=None):
            r = ref(ab, p, q, d)
            return send(r, r, (axis, way), xsem, (phase, ab, sem))

        def spread(ab, j):
            a, b = first[ab], second[ab]
            for d, way in enumerate((1, -1)):
                chunks[ab, "b", j, d] = go(ab, spot(a, j), me[b], b, way, 3 + 4 * j + d)

        def begin(ab):
            a = first[ab]
            if phase == 1:
                for c in range(SLOTS):
                    ring_step(ab, LEAPS, c)
            for d, way in enumerate((1, -1, 2)):
                chunks[ab, "a", d] = go(ab, me[a], me[second[ab]], a, way, d)

        def pass_on(ab, d):
            chunks[ab, "a", d].wait_recv()
            spread(ab, (3, 1, 2)[d])

        def pass_second(ab, j):
            a, b = first[ab], second[ab]
            for d, way in enumerate((1, -1)):
                chunks[ab, "b", j, d].wait_recv()
                chunks[ab, "b2", j, d] = go(ab, spot(a, j), spot(b, -way), b, way, 5 + 4 * j + d, d)

        def share(ab, j):
            for d in range(2):
                chunks[ab, "b2", j, d].wait_recv()
            p = spot(first[ab], j)
            src = store.at[ab, k, p] if ab == 0 else store.at[ab, k, :, p]
            chunks[ab, "c", j] = send(src, src, ("k", 1), dsem, (phase, ab, j))

        def finish(ab, j):
            chunks[ab, "c", j].wait_recv()

        order = [
            (0.0, begin), (0.01, lambda ab: spread(ab, 0)),
            (4.5, lambda ab: pass_on(ab, 0)), (4.5, lambda ab: pass_on(ab, 1)),
            (9.0, lambda ab: pass_on(ab, 2)), (9.1, lambda ab: pass_second(ab, 0)),
            (12.5, lambda ab: pass_second(ab, 3)), (14.7, lambda ab: pass_second(ab, 1)),
            (15.8, lambda ab: share(ab, 0)), (18.1, lambda ab: share(ab, 3)),
            (18.2, lambda ab: pass_second(ab, 2)), (20.4, lambda ab: share(ab, 1)), (22.6, lambda ab: share(ab, 2)),
        ]
        for j in range(4):
            order.append((24.0 if phase == 0 else 1000.0, lambda ab, j=j: finish(ab, j)))
        for at, step in order:
            for ab in range(2):
                events.append((start + at, functools.partial(step, ab)))

    for copy in local:
        copy.wait()
    plane(0, near, 0.0)
    plane(1, far, T_FAR)

    first_row = lax.axis_index("row") * WIDTH + lax.axis_index("layer") * 2

    def held(block_row, group, slot):
        return table[(slot * GROUPS + group) * NB + block_row]

    def left_side(i, half, h, g4):
        free = jnp.zeros((B, 128 - B), jnp.bfloat16)
        for t in range(SLOTS):
            high, low = split(unpack(line[zh * NZL + h * QUAD + g4, i, t]))
            lanes = pl.ds(pl.multiple_of((g4 * SLOTS + t) * 128, 128), 128)
            lhs[i, half, 0:B, lanes] = jnp.concatenate([high, free], axis=1)
            lhs[i, half, B:2 * B, lanes] = jnp.concatenate([low, free], axis=1)

    def right_side(slots, i, half, h, g4):
        store = near if half == 0 else far
        block_row = first_row + i
        group = h * QUAD + g4
        wanted = {s: held(block_row, zl, s) for s in slots}
        for t in range(SLOTS):
            col = held(block_row, group, t)
            inner = jnp.maximum(col, 0)
            cols = [held(group * WIDTH + inner, zl, u) for u in range(SLOTS)]
            depth = pl.ds(pl.multiple_of((g4 * SLOTS + t) * 128, 128), B)
            for s in slots:
                want = jnp.where(col >= 0, wanted[s] + 1, 0)
                hits = [jnp.where(cols[u] + 1 == want, 1, 0) * jnp.where(want > 0, 1, 0) for u in range(SLOTS)]
                u = jnp.minimum(hits[1] + 2 * hits[2], SLOTS - 1)
                on = jnp.minimum(hits[0] + hits[1] + hits[2], 1).astype(jnp.float32)
                block = store[inner & 1, (inner >> 1) & 1, g4, inner >> 2, u] * on
                high, low = split(unpack(block))
                rhs_hi[i, half, depth, s * 128:s * 128 + B] = high
                rhs_lo[i, half, depth, s * 128:s * 128 + B] = low

    def multiply(slots, i, half):
        dot = functools.partial(jnp.dot, preferred_element_type=jnp.float32)
        lanes = slice(slots[0] * 128, (slots[-1] + 1) * 128)
        main = dot(lhs[i, half], rhs_hi[i, half, :, lanes])
        rest = dot(lhs[i, half, 0:B, :], rhs_lo[i, half, :, lanes])
        value = main[0:B] + (main[B:] + rest)
        for n, s in enumerate(slots):
            part = value[:, n * 128:n * 128 + B]
            if half == 0:
                out_ref[i, 0, s] = part
            else:
                out_ref[i, 0, s] += part

    def prepare():
        for ref in (rhs_hi, rhs_lo):
            for i in range(2):
                for half in range(2):
                    for n in range(QUAD * SLOTS):
                        ref[i, half, n * 128 + B:(n + 1) * 128, :] = jnp.zeros((128 - B, SLOTS * 128), jnp.bfloat16)

    def every(fn, half, h):
        def step(n, _):
            fn(n // QUAD, half, h, n % QUAD)
            return 0
        lax.fori_loop(0, 2 * QUAD, step, 0)

    diagonal = lax.axis_index("row") == lax.axis_index("col")
    holds = zh == zl // NX
    n_yk = NY * NK
    mine = y * NK + k

    def plane_copy(j):
        dx, t = (2, 1, 3, 0)[j // n_yk], (mine + j % n_yk) % n_yk
        to = {"x": (x + dx) % NX, "y": t // NK, "k": t % NK, "zh": zh, "zl": zl}
        return pltpu.make_async_remote_copy(
            src_ref=one, dst_ref=in_plane.at[mine], send_sem=psem.at[0, j], recv_sem=psem.at[1, j],
            device_id=device(to), device_id_type=MESH)

    plane_copies = [plane_copy(j) for j in range(NX * n_yk) if j != 3 * n_yk]
    z_copies = {j: pltpu.make_async_remote_copy(
        src_ref=two, dst_ref=along.at[zl], send_sem=zsem.at[0, j], recv_sem=zsem.at[1, j],
        device_id=device(moved(me, "z", j)), device_id_type=MESH)
        for j in sorted(range(1, NZ), key=lambda j: -min(j, NZ - j))}

    def diagonal_sum():
        eye = lax.broadcasted_iota(jnp.int32, (B, B), 0) == lax.broadcasted_iota(jnp.int32, (B, B), 1)
        total = jnp.sum(jnp.where(eye, out_ref[0, 0, 0] + out_ref[1, 0, 0], 0.0))
        return jnp.full((8, 128), total, jnp.float32)

    def to_plane():
        for copy in plane_copies:
            copy.start()
        in_plane[mine] = one[...]

    def to_line():
        dx_in = (x - zl % NX + NX) % NX
        for n, dx in enumerate((2, 1, 3, 0)):
            @pl.when(dx_in == dx)
            def _():
                for t in range(n_yk):
                    if dx != 0 or t != 0:
                        plane_copies[n * n_yk + t - (dx == 0)].wait_recv()
        two[...] = jnp.sum(in_plane[...], axis=0)
        for copy in z_copies.values():
            copy.start()
        along[zl] = two[...]

    other = 1 - zh
    first, rest, whole = (0,), (1, 2), (0, 1, 2)

    def early_trace():
        @pl.when(diagonal)
        def _():
            every(left_side, 0, zh)
            for i in range(2):
                multiply(first, i, 0)
            near_sum[...] = diagonal_sum()

            @pl.when(zh == 1)
            def _():
                one[...] = near_sum[...]
                to_plane()

    events.append((0.3, prepare))
    events.append((AT_NEAR, lambda: every(functools.partial(right_side, whole), 0, zh)))
    events.append((AT_TRACE, early_trace))
    events.append((AT_TRACE + 3.0, lambda: pl.when(jnp.logical_and(holds, zh == 1))(to_line)))
    events.append((AT_LEFT, lambda: every(left_side, 0, zh)))
    events.append((AT_LEFT + 0.5, lambda: every(left_side, 1, other)))
    for i in range(2):
        events.append((AT_LEFT + 1.0 + i, functools.partial(multiply, whole, i, 0)))
    for _, step in sorted(events, key=lambda e: e[0]):
        step()

    def far_products(slots):
        every(functools.partial(right_side, slots), 1, other)
        for i in range(2):
            multiply(slots, i, 1)

    far_products(first)

    @pl.when(jnp.logical_and(diagonal, zh == 0))
    def _():
        one[...] = 2.0 * diagonal_sum() - near_sum[...]
        to_plane()

    far_products(rest)
    pl.when(jnp.logical_and(holds, zh == 0))(to_line)

    for j, copy in z_copies.items():
        from_z = ups[-j % NZ]
        pl.when(from_z // NZL == from_z % NZL // NX)(copy.wait_recv)
    trace_ref[0, 0] = jnp.sum(along[:, 0:1, 0:1])

    @pl.when(holds)
    def _():
        for copy in z_copies.values():
            copy.wait_send()

    @pl.when(diagonal)
    def _():
        for copy in plane_copies:
            copy.wait_send()

    for copy, when in sent:
        if when is None:
            copy.wait_send()
        else:
            pl.when(when)(copy.wait_send)


def square(table, blocks, collective_id=0, name="square"):
    return pl.pallas_call(
        kernel,
        out_shape=(jax.ShapeDtypeStruct((2, 1, SLOTS, B, B), jnp.float32), jax.ShapeDtypeStruct((1, 1), jnp.float32)),
        in_specs=[pl.BlockSpec(memory_space=pltpu.SMEM), pl.BlockSpec(memory_space=pl.ANY)],
        out_specs=(pl.BlockSpec(memory_space=pltpu.VMEM), pl.BlockSpec(memory_space=pltpu.SMEM)),
        scratch_shapes=[
            pltpu.VMEM((2, 1, SLOTS, B, B), jnp.float32),
            pltpu.VMEM((2, SLOTS, PACK, 128), jnp.float32),
            pltpu.VMEM((NZ, 2, SLOTS, PACK, 128), jnp.float32),
            pltpu.VMEM((2, NK, NX, NY, SLOTS, PACK, 128), jnp.float32),
            pltpu.VMEM((2, NK, NX, NY, SLOTS, PACK, 128), jnp.float32),
            pltpu.VMEM((2, 2, 2 * B, DEPTH), jnp.bfloat16),
            pltpu.VMEM((2, 2, DEPTH, SLOTS * 128), jnp.bfloat16),
            pltpu.VMEM((2, 2, DEPTH, SLOTS * 128), jnp.bfloat16),
            pltpu.VMEM((NY * NK, 8, 128), jnp.float32),
            pltpu.VMEM((NZL, 8, 128), jnp.float32),
            pltpu.VMEM((8, 128), jnp.float32),
            pltpu.VMEM((8, 128), jnp.float32),
            pltpu.VMEM((8, 128), jnp.float32),
            pltpu.SemaphoreType.DMA((3,)),
            pltpu.SemaphoreType.DMA((2, 2, NZL, SLOTS)),
            pltpu.SemaphoreType.DMA((2, 2, NZL, SLOTS)),
            pltpu.SemaphoreType.DMA((2, 2, 2, 20)),
            pltpu.SemaphoreType.DMA((2, 2, 2, 4)),
            pltpu.SemaphoreType.DMA((2, NX * NY * NK)),
            pltpu.SemaphoreType.DMA((2, NZ)),
        ],
        compiler_params=pltpu.CompilerParams(collective_id=collective_id, has_side_effects=True, vmem_limit_bytes=48 << 20),
        name=name,
    )(table, blocks)


def body(blocks, block_cols, occupancy):
    table = jnp.where(occupancy == 1, block_cols, -1).transpose(2, 1, 0).reshape(-1)
    product, trace = square(table, blocks)
    return product, trace[0, 0]


def solution(mesh):
    in_specs = (P(("row", "layer"), "col", None, None, None), P(), P())
    out_specs = (P(("row", "layer"), "col", None, None, None), P())
    return jax.shard_map(body, mesh=mesh, in_specs=in_specs, out_specs=out_specs, check_vma=False)
```

```python
import functools

import jax
import jax.numpy as jnp
from jax import lax
from jax.experimental import pallas as pl
from jax.experimental.pallas import tpu as pltpu
from jax.sharding import PartitionSpec as P

MESH = pl.DeviceIdType.MESH
NX, NY, NZH, NZL, NK = 4, 4, 2, 8, 2
NZ = NZH * NZL
LEAPS = NZL // 2
B, SLOTS, PACK = 96, 3, 72
CUT = 32
NB, GROUPS, WIDTH = 128, 8, 16
QUAD = GROUPS // NZH
DEPTH = QUAD * SLOTS * 128

T_RING, T_OWN, T_TAIL0, T_TAIL, T_SIDE0, T_SIDE, T_FAR = 3.6, 13.0, 14.0, 3.0, 18.0, 2.0, 16.0
AT_NEAR, AT_TRACE, AT_LEFT = 24.5, 30.0, 37.0


def here():
    r, c, l = lax.axis_index("row"), lax.axis_index("col"), lax.axis_index("layer")
    return {"x": r % NX, "zh": r // NX, "zl": c, "y": l // NK, "k": l % NK}


def device(at):
    return {"row": at["zh"] * NX + at["x"], "col": at["zl"], "layer": at["y"] * NK + at["k"]}


def moved(at, axis, by):
    at = dict(at)
    if axis == "x":
        at["x"] = (at["x"] + by + NX) % NX
    elif axis == "y":
        at["y"] = (at["y"] + by + NY) % NY
    elif axis == "k":
        at["k"] = 1 - at["k"]
    else:
        z = (at["zh"] * NZL + at["zl"] + by + NZ) % NZ
        at["zh"], at["zl"] = z // NZL, z % NZL
    return at


def pack(block):
    rest = block[PACK:, :]
    side = jnp.concatenate([rest[:, 0:32], rest[:, 32:64], rest[:, 64:96]], axis=0)
    return jnp.concatenate([block[:PACK, :], side], axis=1)


def unpack(packed):
    side = packed[:, B:]
    rest = jnp.concatenate([side[0:24], side[24:48], side[48:72]], axis=1)
    return jnp.concatenate([packed[:, :B], rest], axis=0)


def split(value):
    high = value.astype(jnp.bfloat16)
    return high, (value - high.astype(jnp.float32)).astype(jnp.bfloat16)


def kernel(table, b_ref, out_ref, trace_ref, raw, own, line, near, far, lhs, rhs_hi, rhs_lo, in_plane, along, one, two, near_sum,
           ruler,
           lsem, ring_in, side_in, tail_in, plane_in, share_in, small_in, out_sem, side_out, tail_out):
    me = here()
    zl, zh, x, y, k = me["zl"], me["zh"], me["x"], me["y"], me["k"]
    z = zh * NZL + zl
    steps = [("z", 1), ("z", -1), ("z", 2), ("z", -2), ("x", 1), ("x", -1), ("x", 2), ("y", 1), ("y", -1), ("y", 2), ("k", 1)]
    near_by = {step: moved(me, *step) for step in steps}
    ids = {step: device(at) for step, at in near_by.items()}
    spots = {(axis, by): near_by[axis, by if by < 3 else -1][axis] if by else me[axis] for axis in ("x", "y") for by in range(4)}
    ups = [(z + j) % NZ for j in range(NZ)]
    barrier = pltpu.get_barrier_semaphore()
    for step in steps:
        pl.semaphore_signal(barrier, inc=1, device_id=ids[step], device_id_type=MESH)
    load = pltpu.make_async_copy(b_ref, raw, lsem.at[0])
    load.start()
    load.wait()
    for i in range(2):
        for s in range(SLOTS):
            own[i, s] = pack(raw[i, 0, s])
    local = [
        pltpu.make_async_copy(own, line.at[z], lsem.at[1]),
        pltpu.make_async_copy(own.at[0], near.at[0, k, x, y], lsem.at[2]),
        pltpu.make_async_copy(own.at[1], near.at[1, k, x, y], lsem.at[3]),
    ]
    for copy in local:
        copy.start()
    pl.semaphore_wait(barrier, len(steps))

    def send(src, dst, to, out, into, when=None):
        copy = pltpu.make_async_remote_copy(
            src_ref=src, dst_ref=dst, send_sem=out, recv_sem=into, device_id=ids[to], device_id_type=MESH)
        if when is None:
            copy.start()
        else:
            pl.when(when)(copy.start)
        return copy

    def drain(sem, view, when=None):
        def wait():
            pltpu.make_async_copy(view, view, sem).wait()
        if when is None:
            wait()
        else:
            pl.when(when)(wait)

    three, six = line.at[0, 0], line.at[0]
    after = []

    events = []

    ring, tail = {}, {}

    def ring_step(d, m, c):
        way = 1 - 2 * d
        origin = ups[-way * 2 * m % NZ]
        if m > 0:
            ring[d, m - 1, c].wait_recv()
        if m < LEAPS:
            src = own.at[d, c] if m == 0 else line.at[origin, d, c]
            dst = line.at[origin, d, c] if m < LEAPS - 1 else far.at[d, k, x, y, c]
            ring[d, m, c] = send(src, dst, ("z", 2 * way), out_sem.at[0], ring_in.at[d, m, c])

    def side_send(d, m, c):
        way = 1 - 2 * d
        origin, to = ups[-way * 2 * m % NZ], ups[way % NZ]
        src = own.at[d, c] if m == 0 else line.at[origin, d, c]
        when = origin // NZL == to // NZL
        send(src, line.at[origin, d, c], ("z", way), side_out.at[d, m], side_in.at[d, m], when)
        if c == SLOTS - 1:
            after.append((side_out.at[d, m], three, when))

    def side_wait(d, m):
        way = 1 - 2 * d
        drain(side_in.at[d, m], three, ups[-way * (2 * m + 1) % NZ] // NZL == zh)

    def tail_step(d, n, c):
        way = 1 - 2 * d
        part = 1 - d
        piece = jnp.clip(zl - way * n, 0, NZL - 1)
        origin = zh * NZL + piece
        got = (zl >= n) if d == 0 else (zl + n < NZL)
        more = (zl < NZL - 1) if d == 0 else (zl > 0)
        if n > 0:
            pl.when(got)(tail[d, n - 1, c].wait_recv)
        if n < NZL - 1:
            src = own.at[part, c] if n == 0 else line.at[origin, part, c]
            when = jnp.logical_and(got, more)
            tail[d, n, c] = send(src, line.at[origin, part, c], ("z", way), tail_out.at[d, n], tail_in.at[d, n, c], when)
            if c == SLOTS - 1:
                after.append((tail_out.at[d, n], three, when))

    for c in range(SLOTS):
        for d in range(2):
            for m in range(LEAPS):
                events.append((T_RING * m + 0.76 * c, functools.partial(ring_step, d, m, c)))
                events.append((T_SIDE0 + T_SIDE * m + 0.76 * c, functools.partial(side_send, d, m, c)))
                if c == SLOTS - 1:
                    events.append((T_SIDE0 + T_SIDE * m + 8.0 + 0.76 * c, functools.partial(side_wait, d, m)))
            for n in range(NZL):
                events.append((T_OWN if n == 0 else T_TAIL0 + T_TAIL * n + 0.76 * c, functools.partial(tail_step, d, n, c)))

    def plane(phase, store, start):
        first, second = ("x", "y"), ("y", "x")

        def ref(ab, p, q, d=None):
            view = store.at[ab, k, p, q] if ab == 0 else store.at[ab, k, q, p]
            if d is None:
                return view
            low = CUT if ab == 0 else PACK - CUT
            return view.at[:, pl.ds(0, low)] if d == 0 else view.at[:, pl.ds(low, PACK - low)]

        def spot(axis, by):
            return spots[axis, by % 4]

        def go(ab, p, q, axis, way, sem, d=None):
            r = ref(ab, p, q, d)
            send(r, r, (axis, way), out_sem.at[1 + phase], plane_in.at[phase, ab, sem])

        def spread(ab, j):
            a, b = first[ab], second[ab]
            for way in (1, -1):
                go(ab, spot(a, j), me[b], b, way, 3 + j)

        def begin(ab):
            a = first[ab]
            if phase == 1:
                for c in range(SLOTS):
                    ring_step(ab, LEAPS, c)
            for d, way in enumerate((1, -1, 2)):
                go(ab, me[a], me[second[ab]], a, way, d)

        def pass_on(ab, d):
            drain(plane_in.at[phase, ab, d], three)
            spread(ab, (3, 1, 2)[d])

        def pass_second(ab, j):
            a, b = first[ab], second[ab]
            drain(plane_in.at[phase, ab, 3 + j], six)
            for d, way in enumerate((1, -1)):
                go(ab, spot(a, j), spot(b, -way), b, way, 7 + j, d)

        def share(ab, j):
            drain(plane_in.at[phase, ab, 7 + j], three)
            p = spot(first[ab], j)
            src = store.at[ab, k, p] if ab == 0 else store.at[ab, k, :, p]
            send(src, src, ("k", 1), out_sem.at[3 + phase], share_in.at[phase])

        order = [
            (0.0, begin), (0.01, lambda ab: spread(ab, 0)),
            (4.5, lambda ab: pass_on(ab, 0)), (4.5, lambda ab: pass_on(ab, 1)),
            (9.0, lambda ab: pass_on(ab, 2)), (9.1, lambda ab: pass_second(ab, 0)),
            (12.5, lambda ab: pass_second(ab, 3)), (14.7, lambda ab: pass_second(ab, 1)),
            (15.8, lambda ab: share(ab, 0)), (18.1, lambda ab: share(ab, 3)),
            (18.2, lambda ab: pass_second(ab, 2)), (20.4, lambda ab: share(ab, 1)), (22.6, lambda ab: share(ab, 2)),
        ]
        for at, step in order:
            for ab in range(2):
                events.append((start + at, functools.partial(step, ab)))
        events.append((start + 24.0 if phase == 0 else 1000.0, lambda: drain(share_in.at[phase], line)))
        after.append((out_sem.at[1 + phase], line.at[pl.ds(0, 15)], None))
        after.append((out_sem.at[3 + phase], line, None))

    for copy in local:
        copy.wait()
    plane(0, near, 0.0)
    plane(1, far, T_FAR)

    first_row = lax.axis_index("row") * WIDTH + lax.axis_index("layer") * 2

    def held(block_row, group, slot):
        return table[(slot * GROUPS + group) * NB + block_row]

    def left_side(i, half, h, g4):
        free = jnp.zeros((B, 128 - B), jnp.bfloat16)
        for t in range(SLOTS):
            high, low = split(unpack(line[zh * NZL + h * QUAD + g4, i, t]))
            lanes = pl.ds(pl.multiple_of((g4 * SLOTS + t) * 128, 128), 128)
            lhs[i, half, 0:B, lanes] = jnp.concatenate([high, free], axis=1)
            lhs[i, half, B:2 * B, lanes] = jnp.concatenate([low, free], axis=1)

    def right_side(slots, i, half, h, g4):
        store = near if half == 0 else far
        block_row = first_row + i
        group = h * QUAD + g4
        wanted = {s: held(block_row, zl, s) for s in slots}
        for t in range(SLOTS):
            col = held(block_row, group, t)
            inner = jnp.maximum(col, 0)
            cols = [held(group * WIDTH + inner, zl, u) for u in range(SLOTS)]
            depth = pl.ds(pl.multiple_of((g4 * SLOTS + t) * 128, 128), B)
            for s in slots:
                want = jnp.where(col >= 0, wanted[s] + 1, 0)
                hits = [jnp.where(cols[u] + 1 == want, 1, 0) * jnp.where(want > 0, 1, 0) for u in range(SLOTS)]
                u = jnp.minimum(hits[1] + 2 * hits[2], SLOTS - 1)
                on = jnp.minimum(hits[0] + hits[1] + hits[2], 1).astype(jnp.float32)
                block = store[inner & 1, (inner >> 1) & 1, g4, inner >> 2, u] * on
                high, low = split(unpack(block))
                rhs_hi[i, half, depth, s * 128:s * 128 + B] = high
                rhs_lo[i, half, depth, s * 128:s * 128 + B] = low

    def multiply(slots, i, half):
        dot = functools.partial(jnp.dot, preferred_element_type=jnp.float32)
        lanes = slice(slots[0] * 128, (slots[-1] + 1) * 128)
        main = dot(lhs[i, half], rhs_hi[i, half, :, lanes])
        rest = dot(lhs[i, half, 0:B, :], rhs_lo[i, half, :, lanes])
        value = main[0:B] + (main[B:] + rest)
        for n, s in enumerate(slots):
            part = value[:, n * 128:n * 128 + B]
            if half == 0:
                out_ref[i, 0, s] = part
            else:
                out_ref[i, 0, s] += part

    def prepare():
        for ref in (rhs_hi, rhs_lo):
            for i in range(2):
                for half in range(2):
                    for n in range(QUAD * SLOTS):
                        ref[i, half, n * 128 + B:(n + 1) * 128, :] = jnp.zeros((128 - B, SLOTS * 128), jnp.bfloat16)

    def every(fn, half, h):
        def step(n, _):
            fn(n // QUAD, half, h, n % QUAD)
            return 0
        lax.fori_loop(0, 2 * QUAD, step, 0)

    diagonal = lax.axis_index("row") == lax.axis_index("col")
    holds = zh == zl // NX
    n_yk = NY * NK
    mine = y * NK + k

    def plane_copy(j):
        dx, t = (2, 1, 3, 0)[j // n_yk], (mine + j % n_yk) % n_yk
        to = {"x": (x + dx) % NX, "y": t // NK, "k": t % NK, "zh": zh, "zl": zl}
        return pltpu.make_async_remote_copy(
            src_ref=one, dst_ref=in_plane.at[mine], send_sem=out_sem.at[5], recv_sem=small_in.at[0],
            device_id=device(to), device_id_type=MESH)

    plane_copies = [plane_copy(j) for j in range(NX * n_yk) if j != 3 * n_yk]
    z_copies = {j: pltpu.make_async_remote_copy(
        src_ref=two, dst_ref=along.at[zl], send_sem=out_sem.at[6], recv_sem=small_in.at[1],
        device_id=device(moved(me, "z", j)), device_id_type=MESH)
        for j in sorted(range(1, NZ), key=lambda j: -min(j, NZ - j))}

    def diagonal_sum():
        eye = lax.broadcasted_iota(jnp.int32, (B, B), 0) == lax.broadcasted_iota(jnp.int32, (B, B), 1)
        total = jnp.sum(jnp.where(eye, out_ref[0, 0, 0] + out_ref[1, 0, 0], 0.0))
        return jnp.full((8, 128), total, jnp.float32)

    def to_plane():
        for copy in plane_copies:
            copy.start()
        in_plane[mine] = one[...]

    def to_line():
        drain(small_in.at[0], ruler.at[pl.ds(0, n_yk)], jnp.logical_not(diagonal))
        drain(small_in.at[0], ruler.at[pl.ds(0, n_yk - 1)], diagonal)
        two[...] = jnp.sum(in_plane[...], axis=0)
        for copy in z_copies.values():
            copy.start()
        along[zl] = two[...]

    other = 1 - zh
    first, rest, whole = (0,), (1, 2), (0, 1, 2)

    def early_trace():
        @pl.when(diagonal)
        def _():
            every(left_side, 0, zh)
            for i in range(2):
                multiply(first, i, 0)
            near_sum[...] = diagonal_sum()

            @pl.when(zh == 1)
            def _():
                one[...] = near_sum[...]
                to_plane()

    events.append((0.3, prepare))
    events.append((AT_NEAR, lambda: every(functools.partial(right_side, whole), 0, zh)))
    events.append((AT_TRACE, early_trace))
    events.append((AT_TRACE + 3.0, lambda: pl.when(jnp.logical_and(holds, zh == 1))(to_line)))
    events.append((AT_LEFT, lambda: every(left_side, 0, zh)))
    events.append((AT_LEFT + 0.5, lambda: every(left_side, 1, other)))
    for i in range(2):
        events.append((AT_LEFT + 1.0 + i, functools.partial(multiply, whole, i, 0)))
    for _, step in sorted(events, key=lambda e: e[0]):
        step()

    def far_products(slots):
        every(functools.partial(right_side, slots), 1, other)
        for i in range(2):
            multiply(slots, i, 1)

    far_products(first)

    @pl.when(jnp.logical_and(diagonal, zh == 0))
    def _():
        one[...] = 2.0 * diagonal_sum() - near_sum[...]
        to_plane()

    far_products(rest)
    pl.when(jnp.logical_and(holds, zh == 0))(to_line)

    drain(small_in.at[1], ruler.at[pl.ds(0, NZL)], jnp.logical_not(holds))
    drain(small_in.at[1], ruler.at[pl.ds(0, NZL - 1)], holds)
    trace_ref[0, 0] = jnp.sum(along[:, 0:1, 0:1])

    drain(out_sem.at[5], ruler.at[pl.ds(0, NX * n_yk - 1)], diagonal)
    drain(out_sem.at[6], ruler.at[pl.ds(0, NZ - 1)], holds)
    drain(out_sem.at[0], line.at[pl.ds(0, LEAPS)])
    for sem, view, when in after:
        drain(sem, view, when)


def square(table, blocks, collective_id=0, name="square"):
    return pl.pallas_call(
        kernel,
        out_shape=(jax.ShapeDtypeStruct((2, 1, SLOTS, B, B), jnp.float32), jax.ShapeDtypeStruct((1, 1), jnp.float32)),
        in_specs=[pl.BlockSpec(memory_space=pltpu.SMEM), pl.BlockSpec(memory_space=pl.ANY)],
        out_specs=(pl.BlockSpec(memory_space=pltpu.VMEM), pl.BlockSpec(memory_space=pltpu.SMEM)),
        scratch_shapes=[
            pltpu.VMEM((2, 1, SLOTS, B, B), jnp.float32),
            pltpu.VMEM((2, SLOTS, PACK, 128), jnp.float32),
            pltpu.VMEM((NZ, 2, SLOTS, PACK, 128), jnp.float32),
            pltpu.VMEM((2, NK, NX, NY, SLOTS, PACK, 128), jnp.float32),
            pltpu.VMEM((2, NK, NX, NY, SLOTS, PACK, 128), jnp.float32),
            pltpu.VMEM((2, 2, 2 * B, DEPTH), jnp.bfloat16),
            pltpu.VMEM((2, 2, DEPTH, SLOTS * 128), jnp.bfloat16),
            pltpu.VMEM((2, 2, DEPTH, SLOTS * 128), jnp.bfloat16),
            pltpu.VMEM((NY * NK, 8, 128), jnp.float32),
            pltpu.VMEM((NZL, 8, 128), jnp.float32),
            pltpu.VMEM((8, 128), jnp.float32),
            pltpu.VMEM((8, 128), jnp.float32),
            pltpu.VMEM((8, 128), jnp.float32),
            pltpu.VMEM((NX * NY * NK, 8, 128), jnp.float32),
            pltpu.SemaphoreType.DMA((4,)),
            pltpu.SemaphoreType.DMA((2, LEAPS, SLOTS)),
            pltpu.SemaphoreType.DMA((2, LEAPS)),
            pltpu.SemaphoreType.DMA((2, NZL - 1, SLOTS)),
            pltpu.SemaphoreType.DMA((2, 2, 11)),
            pltpu.SemaphoreType.DMA((2,)),
            pltpu.SemaphoreType.DMA((2,)),
            pltpu.SemaphoreType.DMA((7,)),
            pltpu.SemaphoreType.DMA((2, LEAPS)),
            pltpu.SemaphoreType.DMA((2, NZL - 1)),
        ],
        compiler_params=pltpu.CompilerParams(collective_id=collective_id, has_side_effects=True, vmem_limit_bytes=48 << 20),
        name=name,
    )(table, blocks)


def body(blocks, block_cols, occupancy):
    table = jnp.where(occupancy == 1, block_cols, -1).transpose(2, 1, 0).reshape(-1)
    product, trace = square(table, blocks)
    return product, trace[0, 0]


def solution(mesh):
    in_specs = (P(("row", "layer"), "col", None, None, None), P(), P())
    out_specs = (P(("row", "layer"), "col", None, None, None), P())
    return jax.shard_map(body, mesh=mesh, in_specs=in_specs, out_specs=out_specs, check_vma=False)
```

```python
import functools

import jax
import jax.numpy as jnp
from jax import lax
from jax.experimental import pallas as pl
from jax.experimental.pallas import tpu as pltpu
from jax.sharding import PartitionSpec as P

MESH = pl.DeviceIdType.MESH
NX, NY, NZH, NZL, NK = 4, 4, 2, 8, 2
NZ = NZH * NZL
STRIDE = 2
LEAPS = NZL // STRIDE
B, SLOTS, PACK = 96, 3, 72
CUT = 32
NB, GROUPS, WIDTH = 128, 8, 16
QUAD = GROUPS // NZH
DEPTH = QUAD * SLOTS * 128

T_RING, T_OWN, T_TAIL0, T_TAIL, T_SIDE0, T_SIDE, T_FAR = 3.6, 13.0, 14.0, 3.0, 18.0, 2.0, 16.0
AT_NEAR, AT_TRACE, AT_LEFT = 28.0, 32.0, 37.0


def here():
    r, c, l = lax.axis_index("row"), lax.axis_index("col"), lax.axis_index("layer")
    return {"x": r % NX, "zh": r // NX, "zl": c, "y": l // NK, "k": l % NK}


def device(at):
    return {"row": at["zh"] * NX + at["x"], "col": at["zl"], "layer": at["y"] * NK + at["k"]}


def moved(at, axis, by):
    at = dict(at)
    if axis == "x":
        at["x"] = (at["x"] + by + NX) % NX
    elif axis == "y":
        at["y"] = (at["y"] + by + NY) % NY
    elif axis == "k":
        at["k"] = 1 - at["k"]
    else:
        z = (at["zh"] * NZL + at["zl"] + by + NZ) % NZ
        at["zh"], at["zl"] = z // NZL, z % NZL
    return at


def pack(block):
    rest = block[PACK:, :]
    side = jnp.concatenate([rest[:, 0:32], rest[:, 32:64], rest[:, 64:96]], axis=0)
    return jnp.concatenate([block[:PACK, :], side], axis=1)


def unpack(packed):
    side = packed[:, B:]
    rest = jnp.concatenate([side[0:24], side[24:48], side[48:72]], axis=1)
    return jnp.concatenate([packed[:, :B], rest], axis=0)


def split(value):
    high = value.astype(jnp.bfloat16)
    return high, (value - high.astype(jnp.float32)).astype(jnp.bfloat16)


def kernel(table, b_ref, out_ref, trace_ref, own, line, near, far, lhs, rhs_hi, rhs_lo, in_plane, along, one, two, near_sum,
           ruler,
           lsem, ring_in, side_in, tail_in, plane_in, share_in, small_in, out_sem, side_out, tail_out):
    me = here()
    zl, zh, x, y, k = me["zl"], me["zh"], me["x"], me["y"], me["k"]
    z = zh * NZL + zl
    steps = [("z", 1), ("z", -1), ("z", 2), ("z", -2), ("x", 1), ("x", -1), ("x", 2), ("y", 1), ("y", -1), ("y", 2), ("k", 1)]
    near_by = {step: moved(me, *step) for step in steps}
    ids = {step: device(at) for step, at in near_by.items()}
    spots = {(axis, by): near_by[axis, by if by < 3 else -1][axis] if by else me[axis] for axis in ("x", "y") for by in range(4)}
    ups = [(z + j) % NZ for j in range(NZ)]
    barrier = pltpu.get_barrier_semaphore()
    for step in steps:
        pl.semaphore_signal(barrier, inc=1, device_id=ids[step], device_id_type=MESH)
    for i in range(2):
        for s in range(SLOTS):
            own[i, s] = pack(b_ref[i, 0, s])
    local = [
        pltpu.make_async_copy(own, line.at[z], lsem.at[0]),
        pltpu.make_async_copy(own.at[0], near.at[0, k, x, y], lsem.at[1]),
        pltpu.make_async_copy(own.at[1], near.at[1, k, x, y], lsem.at[2]),
    ]
    for copy in local:
        copy.start()
    pl.semaphore_wait(barrier, len(steps))

    def send(src, dst, to, out, into, when=None):
        copy = pltpu.make_async_remote_copy(
            src_ref=src, dst_ref=dst, send_sem=out, recv_sem=into, device_id=ids[to], device_id_type=MESH)
        if when is None:
            copy.start()
        else:
            pl.when(when)(copy.start)
        return copy

    def drain(sem, view, when=None):
        def wait():
            pltpu.make_async_copy(view, view, sem).wait()
        if when is None:
            wait()
        else:
            pl.when(when)(wait)

    three, six = line.at[0, 0], line.at[0]
    after = []

    events = []

    ring, tail = {}, {}

    def ring_step(d, m, c):
        way = 1 - 2 * d
        origin = ups[-way * STRIDE * m % NZ]
        if m > 0:
            ring[d, m - 1, c].wait_recv()
        if m < LEAPS:
            src = own.at[d, c] if m == 0 else line.at[origin, d, c]
            dst = line.at[origin, d, c] if m < LEAPS - 1 else far.at[d, k, x, y, c]
            ring[d, m, c] = send(src, dst, ("z", STRIDE * way), out_sem.at[0], ring_in.at[d, m, c])

    def side_send(d, m, c):
        way = 1 - 2 * d
        origin, to = ups[-way * 2 * m % NZ], ups[way % NZ]
        src = own.at[d, c] if m == 0 else line.at[origin, d, c]
        when = origin // NZL == to // NZL
        send(src, line.at[origin, d, c], ("z", way), side_out.at[d, m], side_in.at[d, m], when)
        if c == SLOTS - 1:
            after.append((side_out.at[d, m], three, when))

    def side_wait(d, m):
        way = 1 - 2 * d
        drain(side_in.at[d, m], three, ups[-way * (2 * m + 1) % NZ] // NZL == zh)

    def tail_step(d, n, c):
        way = 1 - 2 * d
        part = 1 - d
        piece = jnp.clip(zl - way * n, 0, NZL - 1)
        origin = zh * NZL + piece
        got = (zl >= n) if d == 0 else (zl + n < NZL)
        more = (zl < NZL - 1) if d == 0 else (zl > 0)
        if n > 0:
            pl.when(got)(tail[d, n - 1, c].wait_recv)
        if n < NZL - 1:
            src = own.at[part, c] if n == 0 else line.at[origin, part, c]
            when = jnp.logical_and(got, more)
            tail[d, n, c] = send(src, line.at[origin, part, c], ("z", way), tail_out.at[d, n], tail_in.at[d, n, c], when)
            if c == SLOTS - 1:
                after.append((tail_out.at[d, n], three, when))

    for c in range(SLOTS):
        for d in range(2):
            for m in range(LEAPS):
                if m > 0:
                    events.append((T_RING * m + 0.76 * c, functools.partial(ring_step, d, m, c)))
                at = T_SIDE0 + T_SIDE * m + 0.76 * c
                events.append((at, functools.partial(side_send, d, m, c)))
                if c == SLOTS - 1:
                    events.append((at + 8.0, functools.partial(side_wait, d, m)))
            for n in range(NZL):
                events.append((T_OWN if n == 0 else T_TAIL0 + T_TAIL * n + 0.76 * c, functools.partial(tail_step, d, n, c)))

    def plane(phase, store, start):
        first, second = ("x", "y"), ("y", "x")

        def ref(ab, p, q, d=None):
            view = store.at[ab, k, p, q] if ab == 0 else store.at[ab, k, q, p]
            if d is None:
                return view
            low = CUT if ab == 0 else PACK - CUT
            return view.at[:, pl.ds(0, low)] if d == 0 else view.at[:, pl.ds(low, PACK - low)]

        def spot(axis, by):
            return spots[axis, by % 4]

        def go(ab, p, q, axis, way, sem, d=None):
            r = ref(ab, p, q, d)
            send(r, r, (axis, way), out_sem.at[1 + phase], plane_in.at[phase, ab, sem])

        def spread(ab, j):
            a, b = first[ab], second[ab]
            for way in (1, -1):
                go(ab, spot(a, j), me[b], b, way, 3 + j)

        def begin(ab):
            a = first[ab]
            if phase == 1:
                for c in range(SLOTS):
                    ring_step(ab, LEAPS, c)
            for d, way in enumerate((1, -1)):
                go(ab, me[a], me[second[ab]], a, way, d)

        def pass_on(ab, d):
            drain(plane_in.at[phase, ab, d], three)
            if d < 2:
                a, way = first[ab], 1 - 2 * d
                go(ab, spot(a, -way), me[second[ab]], a, way, 2, d)
            spread(ab, (3, 1, 2)[d])

        def pass_second(ab, j):
            a, b = first[ab], second[ab]
            drain(plane_in.at[phase, ab, 3 + j], six)
            for d, way in enumerate((1, -1)):
                go(ab, spot(a, j), spot(b, -way), b, way, 7 + j, d)
            if phase == 1 and j == 2:
                for by in (0, 1, 3):
                    give(ref(ab, spot(a, j), spot(b, by)))

        def give(view):
            send(view, view, ("k", 1), out_sem.at[3 + phase], share_in.at[phase])

        def share(ab, j):
            drain(plane_in.at[phase, ab, 7 + j], three)
            p = spot(first[ab], j)
            if phase == 1 and j == 2:
                give(ref(ab, p, spot(second[ab], 2)))
                return
            give(store.at[ab, k, p] if ab == 0 else store.at[ab, k, :, p])

        order = [
            (0.0, begin), (0.01, lambda ab: spread(ab, 0)),
            (4.5, lambda ab: pass_on(ab, 0)), (4.5, lambda ab: pass_on(ab, 1)),
            (9.0, lambda ab: pass_on(ab, 2)), (9.1, lambda ab: pass_second(ab, 0)),
            (12.5, lambda ab: pass_second(ab, 3)), (14.7, lambda ab: pass_second(ab, 1)),
            (15.8, lambda ab: share(ab, 0)), (18.1, lambda ab: share(ab, 3)),
            (18.2, lambda ab: pass_second(ab, 2)), (20.4, lambda ab: share(ab, 1)), (22.6, lambda ab: share(ab, 2)),
        ]
        for at, step in order:
            for ab in range(2):
                events.append((start + at, functools.partial(step, ab)))
        events.append((start + 24.0 if phase == 0 else 1000.0, lambda: drain(share_in.at[phase], line)))
        after.append((out_sem.at[1 + phase], line.at[pl.ds(0, 15)], None))
        after.append((out_sem.at[3 + phase], line, None))

    for c in range(SLOTS):
        for d in range(2):
            ring_step(d, 0, c)
    for copy in local:
        copy.wait()
    plane(0, near, 0.0)
    plane(1, far, T_FAR)

    first_row = lax.axis_index("row") * WIDTH + lax.axis_index("layer") * 2

    def held(block_row, group, slot):
        return table[(slot * GROUPS + group) * NB + block_row]

    def left_side(i, half, h, g4):
        free = jnp.zeros((B, 128 - B), jnp.bfloat16)
        for t in range(SLOTS):
            high, low = split(unpack(line[zh * NZL + h * QUAD + g4, i, t]))
            lanes = pl.ds(pl.multiple_of((g4 * SLOTS + t) * 128, 128), 128)
            lhs[i, half, 0:B, lanes] = jnp.concatenate([high, free], axis=1)
            lhs[i, half, B:2 * B, lanes] = jnp.concatenate([low, free], axis=1)

    def right_side(slots, i, half, h, g4):
        store = near if half == 0 else far
        block_row = first_row + i
        group = h * QUAD + g4
        wanted = {s: held(block_row, zl, s) for s in slots}
        for t in range(SLOTS):
            col = held(block_row, group, t)
            inner = jnp.maximum(col, 0)
            cols = [held(group * WIDTH + inner, zl, u) for u in range(SLOTS)]
            depth = pl.ds(pl.multiple_of((g4 * SLOTS + t) * 128, 128), B)
            for s in slots:
                want = jnp.where(col >= 0, wanted[s] + 1, 0)
                hits = [jnp.where(cols[u] + 1 == want, 1, 0) * jnp.where(want > 0, 1, 0) for u in range(SLOTS)]
                u = jnp.minimum(hits[1] + 2 * hits[2], SLOTS - 1)
                on = jnp.minimum(hits[0] + hits[1] + hits[2], 1).astype(jnp.float32)
                block = store[inner & 1, (inner >> 1) & 1, g4, inner >> 2, u] * on
                high, low = split(unpack(block))
                rhs_hi[i, half, depth, s * 128:s * 128 + B] = high
                rhs_lo[i, half, depth, s * 128:s * 128 + B] = low

    def multiply(slots, i, half):
        dot = functools.partial(jnp.dot, preferred_element_type=jnp.float32)
        lanes = slice(slots[0] * 128, (slots[-1] + 1) * 128)
        main = dot(lhs[i, half], rhs_hi[i, half, :, lanes])
        rest = dot(lhs[i, half, 0:B, :], rhs_lo[i, half, :, lanes])
        value = main[0:B] + (main[B:] + rest)
        for n, s in enumerate(slots):
            part = value[:, n * 128:n * 128 + B]
            if half == 0:
                out_ref[i, 0, s] = part
            else:
                out_ref[i, 0, s] += part

    def prepare():
        for ref in (rhs_hi, rhs_lo):
            for i in range(2):
                for half in range(2):
                    for n in range(QUAD * SLOTS):
                        ref[i, half, n * 128 + B:(n + 1) * 128, :] = jnp.zeros((128 - B, SLOTS * 128), jnp.bfloat16)

    def every(fn, half, h):
        def step(n, _):
            fn(n // QUAD, half, h, n % QUAD)
            return 0
        lax.fori_loop(0, 2 * QUAD, step, 0)

    diagonal = lax.axis_index("row") == lax.axis_index("col")
    holds = zh == zl // NX
    n_yk = NY * NK
    mine = y * NK + k

    def plane_copy(j):
        dx, t = (2, 1, 3, 0)[j // n_yk], (mine + j % n_yk) % n_yk
        to = {"x": (x + dx) % NX, "y": t // NK, "k": t % NK, "zh": zh, "zl": zl}
        return pltpu.make_async_remote_copy(
            src_ref=one, dst_ref=in_plane.at[mine], send_sem=out_sem.at[5], recv_sem=small_in.at[0],
            device_id=device(to), device_id_type=MESH)

    plane_copies = [plane_copy(j) for j in range(NX * n_yk) if j != 3 * n_yk]
    z_copies = {j: pltpu.make_async_remote_copy(
        src_ref=two, dst_ref=along.at[zl], send_sem=out_sem.at[6], recv_sem=small_in.at[1],
        device_id=device(moved(me, "z", j)), device_id_type=MESH)
        for j in sorted(range(1, NZ), key=lambda j: -min(j, NZ - j))}

    def diagonal_sum():
        eye = lax.broadcasted_iota(jnp.int32, (B, B), 0) == lax.broadcasted_iota(jnp.int32, (B, B), 1)
        total = jnp.sum(jnp.where(eye, out_ref[0, 0, 0] + out_ref[1, 0, 0], 0.0))
        return jnp.full((8, 128), total, jnp.float32)

    def to_plane():
        for copy in plane_copies:
            copy.start()
        in_plane[mine] = one[...]

    def to_line():
        drain(small_in.at[0], ruler.at[pl.ds(0, n_yk)], jnp.logical_not(diagonal))
        drain(small_in.at[0], ruler.at[pl.ds(0, n_yk - 1)], diagonal)
        two[...] = jnp.sum(in_plane[...], axis=0)
        for copy in z_copies.values():
            copy.start()
        along[zl] = two[...]

    other = 1 - zh
    first, rest, whole = (0,), (1, 2), (0, 1, 2)

    def early_trace():
        @pl.when(diagonal)
        def _():
            every(left_side, 0, zh)
            for i in range(2):
                multiply(first, i, 0)
            near_sum[...] = diagonal_sum()

            @pl.when(zh == 1)
            def _():
                one[...] = near_sum[...]
                to_plane()

    events.append((0.3, prepare))
    events.append((AT_NEAR, lambda: every(functools.partial(right_side, whole), 0, zh)))
    events.append((AT_TRACE, early_trace))
    events.append((AT_TRACE + 3.0, lambda: pl.when(jnp.logical_and(holds, zh == 1))(to_line)))
    events.append((AT_LEFT, lambda: every(left_side, 0, zh)))
    events.append((AT_LEFT + 0.5, lambda: every(left_side, 1, other)))
    for i in range(2):
        events.append((AT_LEFT + 1.0 + i, functools.partial(multiply, whole, i, 0)))
    for _, step in sorted(events, key=lambda e: e[0]):
        step()

    def far_products(slots):
        every(functools.partial(right_side, slots), 1, other)
        for i in range(2):
            multiply(slots, i, 1)

    far_products(first)

    @pl.when(jnp.logical_and(diagonal, zh == 0))
    def _():
        one[...] = 2.0 * diagonal_sum() - near_sum[...]
        to_plane()

    far_products(rest)
    pl.when(jnp.logical_and(holds, zh == 0))(to_line)

    drain(small_in.at[1], ruler.at[pl.ds(0, NZL)], jnp.logical_not(holds))
    drain(small_in.at[1], ruler.at[pl.ds(0, NZL - 1)], holds)
    trace_ref[0, 0] = jnp.sum(along[:, 0:1, 0:1])

    drain(out_sem.at[5], ruler.at[pl.ds(0, NX * n_yk - 1)], diagonal)
    drain(out_sem.at[6], ruler.at[pl.ds(0, NZ - 1)], holds)
    drain(out_sem.at[0], line.at[pl.ds(0, LEAPS)])
    for sem, view, when in after:
        drain(sem, view, when)


def square(table, blocks, collective_id=0, name="square"):
    return pl.pallas_call(
        kernel,
        out_shape=(jax.ShapeDtypeStruct((2, 1, SLOTS, B, B), jnp.float32), jax.ShapeDtypeStruct((1, 1), jnp.float32)),
        in_specs=[pl.BlockSpec(memory_space=pltpu.SMEM), pl.BlockSpec(memory_space=pltpu.VMEM)],
        out_specs=(pl.BlockSpec(memory_space=pltpu.VMEM), pl.BlockSpec(memory_space=pltpu.SMEM)),
        scratch_shapes=[
            pltpu.VMEM((2, SLOTS, PACK, 128), jnp.float32),
            pltpu.VMEM((NZ, 2, SLOTS, PACK, 128), jnp.float32),
            pltpu.VMEM((2, NK, NX, NY, SLOTS, PACK, 128), jnp.float32),
            pltpu.VMEM((2, NK, NX, NY, SLOTS, PACK, 128), jnp.float32),
            pltpu.VMEM((2, 2, 2 * B, DEPTH), jnp.bfloat16),
            pltpu.VMEM((2, 2, DEPTH, SLOTS * 128), jnp.bfloat16),
            pltpu.VMEM((2, 2, DEPTH, SLOTS * 128), jnp.bfloat16),
            pltpu.VMEM((NY * NK, 8, 128), jnp.float32),
            pltpu.VMEM((NZL, 8, 128), jnp.float32),
            pltpu.VMEM((8, 128), jnp.float32),
            pltpu.VMEM((8, 128), jnp.float32),
            pltpu.VMEM((8, 128), jnp.float32),
            pltpu.VMEM((NX * NY * NK, 8, 128), jnp.float32),
            pltpu.SemaphoreType.DMA((3,)),
            pltpu.SemaphoreType.DMA((2, LEAPS, SLOTS)),
            pltpu.SemaphoreType.DMA((2, LEAPS)),
            pltpu.SemaphoreType.DMA((2, NZL - 1, SLOTS)),
            pltpu.SemaphoreType.DMA((2, 2, 11)),
            pltpu.SemaphoreType.DMA((2,)),
            pltpu.SemaphoreType.DMA((2,)),
            pltpu.SemaphoreType.DMA((7,)),
            pltpu.SemaphoreType.DMA((2, LEAPS)),
            pltpu.SemaphoreType.DMA((2, NZL - 1)),
        ],
        compiler_params=pltpu.CompilerParams(collective_id=collective_id, has_side_effects=True, vmem_limit_bytes=48 << 20),
        name=name,
    )(table, blocks)


def body(blocks, block_cols, occupancy):
    table = jnp.where(occupancy == 1, block_cols, -1).transpose(2, 1, 0).reshape(-1)
    product, trace = square(table, blocks)
    return product, trace[0, 0]


def solution(mesh):
    in_specs = (P(("row", "layer"), "col", None, None, None), P(), P())
    out_specs = (P(("row", "layer"), "col", None, None, None), P())
    return jax.shard_map(body, mesh=mesh, in_specs=in_specs, out_specs=out_specs, check_vma=False)
```

```python
import functools

import jax
import jax.numpy as jnp
from jax import lax
from jax.experimental import pallas as pl
from jax.experimental.pallas import tpu as pltpu
from jax.sharding import PartitionSpec as P

MESH = pl.DeviceIdType.MESH
NX, NY, NZH, NZL, NK = 4, 4, 2, 8, 2
NZ = NZH * NZL
STRIDE = 2
LEAPS = NZL // STRIDE
B, SLOTS, PACK = 96, 3, 72
CUT = 32
NB, GROUPS, WIDTH = 128, 8, 16
QUAD = GROUPS // NZH
DEPTH = QUAD * SLOTS * 128

T_RING, T_OWN, T_TAIL0, T_TAIL, T_SIDE0, T_SIDE, T_FAR = 3.6, 15.0, 15.5, 3.0, 19.0, 2.0, 16.0
AT_NEAR, AT_TRACE, AT_LEFT = 28.0, 32.0, 39.0


def here():
    r, c, l = lax.axis_index("row"), lax.axis_index("col"), lax.axis_index("layer")
    return {"x": r % NX, "zh": r // NX, "zl": c, "y": l // NK, "k": l % NK}


def device(at):
    return {"row": at["zh"] * NX + at["x"], "col": at["zl"], "layer": at["y"] * NK + at["k"]}


def moved(at, axis, by):
    at = dict(at)
    if axis == "x":
        at["x"] = (at["x"] + by + NX) % NX
    elif axis == "y":
        at["y"] = (at["y"] + by + NY) % NY
    elif axis == "k":
        at["k"] = 1 - at["k"]
    else:
        z = (at["zh"] * NZL + at["zl"] + by + NZ) % NZ
        at["zh"], at["zl"] = z // NZL, z % NZL
    return at


def pack(block):
    rest = block[PACK:, :]
    side = jnp.concatenate([rest[:, 0:32], rest[:, 32:64], rest[:, 64:96]], axis=0)
    return jnp.concatenate([block[:PACK, :], side], axis=1)


def unpack(packed):
    side = packed[:, B:]
    rest = jnp.concatenate([side[0:24], side[24:48], side[48:72]], axis=1)
    return jnp.concatenate([packed[:, :B], rest], axis=0)


def split(value):
    high = value.astype(jnp.bfloat16)
    return high, (value - high.astype(jnp.float32)).astype(jnp.bfloat16)


def kernel(table, b_ref, out_ref, trace_ref, own, line, near, far, lhs, rhs_hi, rhs_lo, in_plane, along, one, two, near_sum,
           ruler,
           lsem, ring_in, side_in, tail_in, plane_in, share_in, small_in, out_sem, side_out, tail_out):
    me = here()
    zl, zh, x, y, k = me["zl"], me["zh"], me["x"], me["y"], me["k"]
    z = zh * NZL + zl
    steps = [("z", 1), ("z", -1), ("z", 2), ("z", -2), ("x", 1), ("x", -1), ("x", 2), ("y", 1), ("y", -1), ("y", 2), ("k", 1)]
    near_by = {step: moved(me, *step) for step in steps}
    ids = {step: device(at) for step, at in near_by.items()}
    spots = {(axis, by): near_by[axis, by if by < 3 else -1][axis] if by else me[axis] for axis in ("x", "y") for by in range(4)}
    ups = [(z + j) % NZ for j in range(NZ)]
    barrier = pltpu.get_barrier_semaphore()
    for step in steps:
        pl.semaphore_signal(barrier, inc=1, device_id=ids[step], device_id_type=MESH)
    for i in range(2):
        for s in range(SLOTS):
            own[i, s] = pack(b_ref[i, 0, s])
    local = [
        pltpu.make_async_copy(own, line.at[z], lsem.at[0]),
        pltpu.make_async_copy(own.at[0], near.at[0, k, x, y], lsem.at[1]),
        pltpu.make_async_copy(own.at[1], near.at[1, k, x, y], lsem.at[2]),
    ]
    for copy in local:
        copy.start()
    pl.semaphore_wait(barrier, len(steps))

    def send(src, dst, to, out, into, when=None):
        copy = pltpu.make_async_remote_copy(
            src_ref=src, dst_ref=dst, send_sem=out, recv_sem=into, device_id=ids[to], device_id_type=MESH)
        if when is None:
            copy.start()
        else:
            pl.when(when)(copy.start)
        return copy

    def drain(sem, view, when=None):
        def wait():
            pltpu.make_async_copy(view, view, sem).wait()
        if when is None:
            wait()
        else:
            pl.when(when)(wait)

    three, six = line.at[0, 0], line.at[0]
    after = []

    events = []

    ring, tail = {}, {}

    def ring_step(d, m, c):
        way = 1 - 2 * d
        origin = ups[-way * STRIDE * m % NZ]
        if m > 0:
            ring[d, m - 1, c].wait_recv()
        if m < LEAPS:
            src = own.at[d, c] if m == 0 else line.at[origin, d, c]
            dst = line.at[origin, d, c] if m < LEAPS - 1 else far.at[d, k, x, y, c]
            ring[d, m, c] = send(src, dst, ("z", STRIDE * way), out_sem.at[0], ring_in.at[d, m, c])

    def side_send(d, m, c):
        way = 1 - 2 * d
        origin, to = ups[-way * 2 * m % NZ], ups[way % NZ]
        src = own.at[d, c] if m == 0 else line.at[origin, d, c]
        when = origin // NZL == to // NZL
        send(src, line.at[origin, d, c], ("z", way), side_out.at[d, m], side_in.at[d, m], when)
        if c == SLOTS - 1:
            after.append((side_out.at[d, m], three, when))

    def side_wait(d, m):
        way = 1 - 2 * d
        drain(side_in.at[d, m], three, ups[-way * (2 * m + 1) % NZ] // NZL == zh)

    def tail_step(d, n, c):
        way = 1 - 2 * d
        part = 1 - d
        piece = jnp.clip(zl - way * n, 0, NZL - 1)
        origin = zh * NZL + piece
        got = (zl >= n) if d == 0 else (zl + n < NZL)
        more = (zl < NZL - 1) if d == 0 else (zl > 0)
        if n > 0:
            pl.when(got)(tail[d, n - 1, c].wait_recv)
        if n < NZL - 1:
            src = own.at[part, c] if n == 0 else line.at[origin, part, c]
            when = jnp.logical_and(got, more)
            tail[d, n, c] = send(src, line.at[origin, part, c], ("z", way), tail_out.at[d, n], tail_in.at[d, n, c], when)
            if c == SLOTS - 1:
                after.append((tail_out.at[d, n], three, when))

    for c in range(SLOTS):
        for d in range(2):
            for m in range(LEAPS):
                if m > 0:
                    events.append((T_RING * m + 0.76 * c, functools.partial(ring_step, d, m, c)))
                at = T_SIDE0 + T_SIDE * m + 0.76 * c
                events.append((at, functools.partial(side_send, d, m, c)))
                if c == SLOTS - 1:
                    events.append((at + 8.0, functools.partial(side_wait, d, m)))
            for n in range(NZL):
                events.append((T_OWN if n == 0 else T_TAIL0 + T_TAIL * n + 0.76 * c, functools.partial(tail_step, d, n, c)))

    def plane(phase, store, start):
        first, second = ("x", "y"), ("y", "x")

        def ref(ab, p, q, d=None):
            view = store.at[ab, k, p, q] if ab == 0 else store.at[ab, k, q, p]
            if d is None:
                return view
            low = CUT if ab == 0 else PACK - CUT
            return view.at[:, pl.ds(0, low)] if d == 0 else view.at[:, pl.ds(low, PACK - low)]

        def spot(axis, by):
            return spots[axis, by % 4]

        def go(ab, p, q, axis, way, sem, d=None):
            r = ref(ab, p, q, d)
            send(r, r, (axis, way), out_sem.at[1 + phase], plane_in.at[phase, ab, sem])

        def spread(ab, j):
            a, b = first[ab], second[ab]
            for way in (1, -1):
                go(ab, spot(a, j), me[b], b, way, 3 + j)

        def begin(ab):
            a = first[ab]
            if phase == 1:
                for c in range(SLOTS):
                    ring_step(ab, LEAPS, c)
            for d, way in enumerate((1, -1)):
                go(ab, me[a], me[second[ab]], a, way, d)

        def pass_on(ab, d):
            drain(plane_in.at[phase, ab, d], three)
            if d < 2:
                a, way = first[ab], 1 - 2 * d
                go(ab, spot(a, -way), me[second[ab]], a, way, 2, d)
            spread(ab, (3, 1, 2)[d])

        def pass_second(ab, j):
            a, b = first[ab], second[ab]
            drain(plane_in.at[phase, ab, 3 + j], six)
            for d, way in enumerate((1, -1)):
                go(ab, spot(a, j), spot(b, -way), b, way, 7 + j, d)
            if phase == 1 and j == 2:
                for by in (0, 1, 3):
                    give(ref(ab, spot(a, j), spot(b, by)))

        def give(view):
            send(view, view, ("k", 1), out_sem.at[3 + phase], share_in.at[phase])

        def share(ab, j):
            drain(plane_in.at[phase, ab, 7 + j], three)
            p = spot(first[ab], j)
            if phase == 1 and j == 2:
                give(ref(ab, p, spot(second[ab], 2)))
                return
            give(store.at[ab, k, p] if ab == 0 else store.at[ab, k, :, p])

        order = [
            (0.0, begin), (0.01, lambda ab: spread(ab, 0)),
            (4.5, lambda ab: pass_on(ab, 0)), (4.5, lambda ab: pass_on(ab, 1)),
            (9.0, lambda ab: pass_on(ab, 2)), (9.1, lambda ab: pass_second(ab, 0)),
            (12.5, lambda ab: pass_second(ab, 3)), (14.7, lambda ab: pass_second(ab, 1)),
            (15.8, lambda ab: share(ab, 0)), (18.1, lambda ab: share(ab, 3)),
            (18.2, lambda ab: pass_second(ab, 2)), (20.4, lambda ab: share(ab, 1)), (22.6, lambda ab: share(ab, 2)),
        ]
        for at, step in order:
            for ab in range(2):
                events.append((start + at, functools.partial(step, ab)))
        events.append((start + 24.0 if phase == 0 else 1000.0, lambda: drain(share_in.at[phase], line)))
        after.append((out_sem.at[1 + phase], line.at[pl.ds(0, 15)], None))
        after.append((out_sem.at[3 + phase], line, None))

    for c in range(SLOTS):
        for d in range(2):
            ring_step(d, 0, c)
    for copy in local:
        copy.wait()
    plane(0, near, 0.0)
    plane(1, far, T_FAR)

    first_row = lax.axis_index("row") * WIDTH + lax.axis_index("layer") * 2

    def held(block_row, group, slot):
        return table[(slot * GROUPS + group) * NB + block_row]

    def left_side(i, half, h, g4):
        free = jnp.zeros((B, 128 - B), jnp.bfloat16)
        for t in range(SLOTS):
            high, low = split(unpack(line[zh * NZL + h * QUAD + g4, i, t]))
            lanes = pl.ds(pl.multiple_of((g4 * SLOTS + t) * 128, 128), 128)
            lhs[i, half, 0:B, lanes] = jnp.concatenate([high, free], axis=1)
            lhs[i, half, B:2 * B, lanes] = jnp.concatenate([low, free], axis=1)

    def right_side(slots, i, half, h, g4):
        store = near if half == 0 else far
        block_row = first_row + i
        group = h * QUAD + g4
        wanted = {s: held(block_row, zl, s) for s in slots}
        for t in range(SLOTS):
            col = held(block_row, group, t)
            inner = jnp.maximum(col, 0)
            cols = [held(group * WIDTH + inner, zl, u) for u in range(SLOTS)]
            depth = pl.ds(pl.multiple_of((g4 * SLOTS + t) * 128, 128), B)
            for s in slots:
                want = jnp.where(col >= 0, wanted[s] + 1, 0)
                hits = [jnp.where(cols[u] + 1 == want, 1, 0) * jnp.where(want > 0, 1, 0) for u in range(SLOTS)]
                u = jnp.minimum(hits[1] + 2 * hits[2], SLOTS - 1)
                on = jnp.minimum(hits[0] + hits[1] + hits[2], 1).astype(jnp.float32)
                block = store[inner & 1, (inner >> 1) & 1, g4, inner >> 2, u] * on
                high, low = split(unpack(block))
                rhs_hi[i, half, depth, s * 128:s * 128 + B] = high
                rhs_lo[i, half, depth, s * 128:s * 128 + B] = low

    def multiply(slots, i, half, added=()):
        dot = functools.partial(jnp.dot, preferred_element_type=jnp.float32)
        lanes = slice(slots[0] * 128, (slots[-1] + 1) * 128)
        main = dot(lhs[i, half], rhs_hi[i, half, :, lanes])
        rest = dot(lhs[i, half, 0:B, :], rhs_lo[i, half, :, lanes])
        value = main[0:B] + (main[B:] + rest)
        for n, s in enumerate(slots):
            part = value[:, n * 128:n * 128 + B]
            if s in added:
                out_ref[i, 0, s] += part
            else:
                out_ref[i, 0, s] = part

    def prepare():
        for ref in (rhs_hi, rhs_lo):
            for i in range(2):
                for half in range(2):
                    for n in range(QUAD * SLOTS):
                        ref[i, half, n * 128 + B:(n + 1) * 128, :] = jnp.zeros((128 - B, SLOTS * 128), jnp.bfloat16)

    def every(fn, half, h):
        def step(n, _):
            fn(n // QUAD, half, h, n % QUAD)
            return 0
        lax.fori_loop(0, 2 * QUAD, step, 0)

    diagonal = lax.axis_index("row") == lax.axis_index("col")
    holds = zh == zl // NX
    n_yk = NY * NK
    mine = y * NK + k

    def plane_copy(j):
        dx, t = (2, 1, 3, 0)[j // n_yk], (mine + j % n_yk) % n_yk
        to = {"x": (x + dx) % NX, "y": t // NK, "k": t % NK, "zh": zh, "zl": zl}
        return pltpu.make_async_remote_copy(
            src_ref=one, dst_ref=in_plane.at[mine], send_sem=out_sem.at[5], recv_sem=small_in.at[0],
            device_id=device(to), device_id_type=MESH)

    plane_copies = [plane_copy(j) for j in range(NX * n_yk) if j != 3 * n_yk]
    z_copies = {j: pltpu.make_async_remote_copy(
        src_ref=two, dst_ref=along.at[zl], send_sem=out_sem.at[6], recv_sem=small_in.at[1],
        device_id=device(moved(me, "z", j)), device_id_type=MESH)
        for j in sorted(range(1, NZ), key=lambda j: -min(j, NZ - j))}

    def diagonal_sum():
        eye = lax.broadcasted_iota(jnp.int32, (B, B), 0) == lax.broadcasted_iota(jnp.int32, (B, B), 1)
        total = jnp.sum(jnp.where(eye, out_ref[0, 0, 0] + out_ref[1, 0, 0], 0.0))
        return jnp.full((8, 128), total, jnp.float32)

    def to_plane():
        for copy in plane_copies:
            copy.start()
        in_plane[mine] = one[...]

    def to_line():
        drain(small_in.at[0], ruler.at[pl.ds(0, n_yk)], jnp.logical_not(diagonal))
        drain(small_in.at[0], ruler.at[pl.ds(0, n_yk - 1)], diagonal)
        two[...] = jnp.sum(in_plane[...], axis=0)
        for copy in z_copies.values():
            copy.start()
        along[zl] = two[...]

    other = 1 - zh
    first, rest, whole = (0,), (1, 2), (0, 1, 2)

    def early_trace():
        @pl.when(diagonal)
        def _():
            every(left_side, 0, zh)
            for i in range(2):
                multiply(first, i, 0)
            near_sum[...] = diagonal_sum()

            @pl.when(zh == 1)
            def _():
                one[...] = near_sum[...]
                to_plane()

    events.append((0.3, prepare))
    events.append((AT_NEAR, lambda: every(functools.partial(right_side, whole), 0, zh)))
    events.append((AT_TRACE, early_trace))
    events.append((AT_TRACE + 3.0, lambda: pl.when(jnp.logical_and(holds, zh == 1))(to_line)))
    events.append((AT_LEFT, lambda: every(left_side, 1, other)))
    for _, step in sorted(events, key=lambda e: e[0]):
        step()

    every(functools.partial(right_side, first), 1, other)
    for i in range(2):
        multiply(first, i, 1)

    @pl.when(jnp.logical_and(diagonal, zh == 0))
    def _():
        one[...] = 2.0 * diagonal_sum() + near_sum[...]
        to_plane()

    every(left_side, 0, zh)
    for i in range(2):
        multiply(whole, i, 0, added=first)
    every(functools.partial(right_side, rest), 1, other)
    for i in range(2):
        multiply(rest, i, 1, added=rest)
    pl.when(jnp.logical_and(holds, zh == 0))(to_line)

    drain(small_in.at[1], ruler.at[pl.ds(0, NZL)], jnp.logical_not(holds))
    drain(small_in.at[1], ruler.at[pl.ds(0, NZL - 1)], holds)
    trace_ref[0, 0] = jnp.sum(along[:, 0:1, 0:1])

    drain(out_sem.at[5], ruler.at[pl.ds(0, NX * n_yk - 1)], diagonal)
    drain(out_sem.at[6], ruler.at[pl.ds(0, NZ - 1)], holds)
    drain(out_sem.at[0], line.at[pl.ds(0, LEAPS)])
    for sem, view, when in after:
        drain(sem, view, when)


def square(table, blocks, collective_id=0, name="square"):
    return pl.pallas_call(
        kernel,
        out_shape=(jax.ShapeDtypeStruct((2, 1, SLOTS, B, B), jnp.float32), jax.ShapeDtypeStruct((1, 1), jnp.float32)),
        in_specs=[pl.BlockSpec(memory_space=pltpu.SMEM), pl.BlockSpec(memory_space=pltpu.VMEM)],
        out_specs=(pl.BlockSpec(memory_space=pltpu.VMEM), pl.BlockSpec(memory_space=pltpu.SMEM)),
        scratch_shapes=[
            pltpu.VMEM((2, SLOTS, PACK, 128), jnp.float32),
            pltpu.VMEM((NZ, 2, SLOTS, PACK, 128), jnp.float32),
            pltpu.VMEM((2, NK, NX, NY, SLOTS, PACK, 128), jnp.float32),
            pltpu.VMEM((2, NK, NX, NY, SLOTS, PACK, 128), jnp.float32),
            pltpu.VMEM((2, 2, 2 * B, DEPTH), jnp.bfloat16),
            pltpu.VMEM((2, 2, DEPTH, SLOTS * 128), jnp.bfloat16),
            pltpu.VMEM((2, 2, DEPTH, SLOTS * 128), jnp.bfloat16),
            pltpu.VMEM((NY * NK, 8, 128), jnp.float32),
            pltpu.VMEM((NZL, 8, 128), jnp.float32),
            pltpu.VMEM((8, 128), jnp.float32),
            pltpu.VMEM((8, 128), jnp.float32),
            pltpu.VMEM((8, 128), jnp.float32),
            pltpu.VMEM((NX * NY * NK, 8, 128), jnp.float32),
            pltpu.SemaphoreType.DMA((3,)),
            pltpu.SemaphoreType.DMA((2, LEAPS, SLOTS)),
            pltpu.SemaphoreType.DMA((2, LEAPS)),
            pltpu.SemaphoreType.DMA((2, NZL - 1, SLOTS)),
            pltpu.SemaphoreType.DMA((2, 2, 11)),
            pltpu.SemaphoreType.DMA((2,)),
            pltpu.SemaphoreType.DMA((2,)),
            pltpu.SemaphoreType.DMA((7,)),
            pltpu.SemaphoreType.DMA((2, LEAPS)),
            pltpu.SemaphoreType.DMA((2, NZL - 1)),
        ],
        compiler_params=pltpu.CompilerParams(collective_id=collective_id, has_side_effects=True, vmem_limit_bytes=48 << 20),
        name=name,
    )(table, blocks)


def body(blocks, block_cols, occupancy):
    table = jnp.where(occupancy == 1, block_cols, -1).transpose(2, 1, 0).reshape(-1)
    product, trace = square(table, blocks)
    return product, trace[0, 0]


def solution(mesh):
    in_specs = (P(("row", "layer"), "col", None, None, None), P(), P())
    out_specs = (P(("row", "layer"), "col", None, None, None), P())
    return jax.shard_map(body, mesh=mesh, in_specs=in_specs, out_specs=out_specs, check_vma=False)
```

```python
import functools

import jax
import jax.numpy as jnp
from jax import lax
from jax.experimental import pallas as pl
from jax.experimental.pallas import tpu as pltpu
from jax.sharding import PartitionSpec as P

MESH = pl.DeviceIdType.MESH
NX, NY, NZH, NZL, NK = 4, 4, 2, 8, 2
NZ = NZH * NZL
STRIDE = 2
LEAPS = NZL // STRIDE
B, SLOTS, PACK = 96, 3, 72
CUT = 32
NB, GROUPS, WIDTH = 128, 8, 16
QUAD = GROUPS // NZH
DEPTH = QUAD * SLOTS * 128

T_RING, T_OWN, T_TAIL0, T_TAIL, T_SIDE0, T_SIDE, T_FAR = 3.6, 15.0, 15.5, 3.0, 19.0, 2.0, 16.0
AT_NEAR, AT_TRACE, AT_LEFT = 28.0, 32.0, 39.0


def here():
    r, c, l = lax.axis_index("row"), lax.axis_index("col"), lax.axis_index("layer")
    return {"x": r % NX, "zh": r // NX, "zl": c, "y": l // NK, "k": l % NK}


def device(at):
    return {"row": at["zh"] * NX + at["x"], "col": at["zl"], "layer": at["y"] * NK + at["k"]}


def moved(at, axis, by):
    at = dict(at)
    if axis == "x":
        at["x"] = (at["x"] + by + NX) % NX
    elif axis == "y":
        at["y"] = (at["y"] + by + NY) % NY
    elif axis == "k":
        at["k"] = 1 - at["k"]
    else:
        z = (at["zh"] * NZL + at["zl"] + by + NZ) % NZ
        at["zh"], at["zl"] = z // NZL, z % NZL
    return at


def pack(block):
    rest = block[PACK:, :]
    side = jnp.concatenate([rest[:, 0:32], rest[:, 32:64], rest[:, 64:96]], axis=0)
    return jnp.concatenate([block[:PACK, :], side], axis=1)


def unpack(packed):
    side = packed[:, B:]
    rest = jnp.concatenate([side[0:24], side[24:48], side[48:72]], axis=1)
    return jnp.concatenate([packed[:, :B], rest], axis=0)


def split(value):
    high = value.astype(jnp.bfloat16)
    return high, (value - high.astype(jnp.float32)).astype(jnp.bfloat16)


def kernel(table, b_ref, out_ref, trace_ref, own, line, near, far, lhs, rhs_hi, rhs_lo, in_plane, along, one, two, near_sum,
           ruler,
           lsem, ring_in, side_in, tail_in, plane_in, share_in, small_in, out_sem, side_out, tail_out):
    me = here()
    zl, zh, x, y, k = me["zl"], me["zh"], me["x"], me["y"], me["k"]
    z = zh * NZL + zl
    steps = [("z", 1), ("z", -1), ("z", 2), ("z", -2), ("x", 1), ("x", -1), ("x", 2), ("y", 1), ("y", -1), ("y", 2), ("k", 1)]
    near_by = {step: moved(me, *step) for step in steps}
    ids = {step: device(at) for step, at in near_by.items()}
    spots = {(axis, by): near_by[axis, by if by < 3 else -1][axis] if by else me[axis] for axis in ("x", "y") for by in range(4)}
    ups = [(z + j) % NZ for j in range(NZ)]
    barrier = pltpu.get_barrier_semaphore()
    for step in steps:
        pl.semaphore_signal(barrier, inc=1, device_id=ids[step], device_id_type=MESH)
    for i in range(2):
        for s in range(SLOTS):
            own[i, s] = pack(b_ref[i, 0, s])
    local = [
        pltpu.make_async_copy(own, line.at[z], lsem.at[0]),
        pltpu.make_async_copy(own.at[0], near.at[0, k, x, y], lsem.at[1]),
        pltpu.make_async_copy(own.at[1], near.at[1, k, x, y], lsem.at[2]),
    ]
    for copy in local:
        copy.start()
    pl.semaphore_wait(barrier, len(steps))

    def send(src, dst, to, out, into, when=None):
        copy = pltpu.make_async_remote_copy(
            src_ref=src, dst_ref=dst, send_sem=out, recv_sem=into, device_id=ids[to], device_id_type=MESH)
        if when is None:
            copy.start()
        else:
            pl.when(when)(copy.start)
        return copy

    def drain(sem, view, when=None):
        def wait():
            pltpu.make_async_copy(view, view, sem).wait()
        if when is None:
            wait()
        else:
            pl.when(when)(wait)

    three, six = line.at[0, 0], line.at[0]
    after = []

    events = []

    ring, tail = {}, {}

    def ring_step(d, m, c):
        way = 1 - 2 * d
        origin = ups[-way * STRIDE * m % NZ]
        if m > 0:
            ring[d, m - 1, c].wait_recv()
        if m < LEAPS:
            src = own.at[d, c] if m == 0 else line.at[origin, d, c]
            dst = line.at[origin, d, c] if m < LEAPS - 1 else far.at[d, k, x, y, c]
            ring[d, m, c] = send(src, dst, ("z", STRIDE * way), out_sem.at[0], ring_in.at[d, m, c])

    def side_send(d, m, c):
        way = 1 - 2 * d
        origin, to = ups[-way * 2 * m % NZ], ups[way % NZ]
        src = own.at[d, c] if m == 0 else line.at[origin, d, c]
        when = origin // NZL == to // NZL
        send(src, line.at[origin, d, c], ("z", way), side_out.at[d, m], side_in.at[d, m], when)
        if c == SLOTS - 1:
            after.append((side_out.at[d, m], three, when))

    def side_wait(d, m):
        way = 1 - 2 * d
        drain(side_in.at[d, m], three, ups[-way * (2 * m + 1) % NZ] // NZL == zh)

    def tail_step(d, n, c):
        way = 1 - 2 * d
        part = 1 - d
        piece = jnp.clip(zl - way * n, 0, NZL - 1)
        origin = zh * NZL + piece
        got = (zl >= n) if d == 0 else (zl + n < NZL)
        more = (zl < NZL - 1) if d == 0 else (zl > 0)
        if n > 0:
            pl.when(got)(tail[d, n - 1, c].wait_recv)
        if n < NZL - 1:
            src = own.at[part, c] if n == 0 else line.at[origin, part, c]
            when = jnp.logical_and(got, more)
            tail[d, n, c] = send(src, line.at[origin, part, c], ("z", way), tail_out.at[d, n], tail_in.at[d, n, c], when)
            if c == SLOTS - 1:
                after.append((tail_out.at[d, n], three, when))

    for c in range(SLOTS):
        for d in range(2):
            for m in range(LEAPS):
                if m > 0:
                    events.append((T_RING * m + 0.76 * c, functools.partial(ring_step, d, m, c)))
                at = T_SIDE0 + T_SIDE * m + 0.76 * c
                events.append((at, functools.partial(side_send, d, m, c)))
                if c == SLOTS - 1:
                    events.append((at + 8.0, functools.partial(side_wait, d, m)))
            for n in range(NZL):
                events.append((T_OWN if n == 0 else T_TAIL0 + T_TAIL * n + 0.76 * c, functools.partial(tail_step, d, n, c)))

    def plane(phase, store, start):
        first, second = ("x", "y"), ("y", "x")

        def ref(ab, p, q, d=None):
            view = store.at[ab, k, p, q] if ab == 0 else store.at[ab, k, q, p]
            if d is None:
                return view
            low = CUT if ab == 0 else PACK - CUT
            return view.at[:, pl.ds(0, low)] if d == 0 else view.at[:, pl.ds(low, PACK - low)]

        def spot(axis, by):
            return spots[axis, by % 4]

        def go(ab, p, q, axis, way, sem, d=None):
            r = ref(ab, p, q, d)
            send(r, r, (axis, way), out_sem.at[1 + phase], plane_in.at[phase, ab, sem])

        def spread(ab, j):
            a, b = first[ab], second[ab]
            for way in (1, -1):
                go(ab, spot(a, j), me[b], b, way, 3 + j)

        def begin(ab):
            a = first[ab]
            if phase == 1:
                for c in range(SLOTS):
                    ring_step(ab, LEAPS, c)
            for d, way in enumerate((1, -1)):
                go(ab, me[a], me[second[ab]], a, way, d)

        def pass_on(ab, d):
            drain(plane_in.at[phase, ab, d], three)
            if d < 2:
                a, way = first[ab], 1 - 2 * d
                go(ab, spot(a, -way), me[second[ab]], a, way, 2, d)
            spread(ab, (3, 1, 2)[d])

        def pass_second(ab, j):
            a, b = first[ab], second[ab]
            drain(plane_in.at[phase, ab, 3 + j], six)
            for d, way in enumerate((1, -1)):
                go(ab, spot(a, j), spot(b, -way), b, way, 7 + j, d)
            if phase == 1 and j in (1, 2):
                for by in (0, 1, 3):
                    give(ref(ab, spot(a, j), spot(b, by)))

        def give(view):
            send(view, view, ("k", 1), out_sem.at[3 + phase], share_in.at[phase])

        def share(ab, j):
            drain(plane_in.at[phase, ab, 7 + j], three)
            p = spot(first[ab], j)
            if phase == 1 and j in (1, 2):
                give(ref(ab, p, spot(second[ab], 2)))
                return
            give(store.at[ab, k, p] if ab == 0 else store.at[ab, k, :, p])

        order = [
            (0.0, begin), (0.01, lambda ab: spread(ab, 0)),
            (4.5, lambda ab: pass_on(ab, 0)), (4.5, lambda ab: pass_on(ab, 1)),
            (9.0, lambda ab: pass_on(ab, 2)), (9.1, lambda ab: pass_second(ab, 0)),
            (12.5, lambda ab: pass_second(ab, 3)), (14.7, lambda ab: pass_second(ab, 1)),
            (15.8, lambda ab: share(ab, 0)), (18.1, lambda ab: share(ab, 3)),
            (18.2, lambda ab: pass_second(ab, 2)), (20.4, lambda ab: share(ab, 1)), (22.6, lambda ab: share(ab, 2)),
        ]
        for at, step in order:
            for ab in range(2):
                events.append((start + at, functools.partial(step, ab)))
        events.append((start + 24.0 if phase == 0 else 1000.0, lambda: drain(share_in.at[phase], line)))
        after.append((out_sem.at[1 + phase], line.at[pl.ds(0, 15)], None))
        after.append((out_sem.at[3 + phase], line, None))

    for c in range(SLOTS):
        for d in range(2):
            ring_step(d, 0, c)
    for copy in local:
        copy.wait()
    plane(0, near, 0.0)
    plane(1, far, T_FAR)

    first_row = lax.axis_index("row") * WIDTH + lax.axis_index("layer") * 2

    def held(block_row, group, slot):
        return table[(slot * GROUPS + group) * NB + block_row]

    def left_side(i, half, h, g4):
        free = jnp.zeros((B, 128 - B), jnp.bfloat16)
        for t in range(SLOTS):
            high, low = split(unpack(line[zh * NZL + h * QUAD + g4, i, t]))
            lanes = pl.ds(pl.multiple_of((g4 * SLOTS + t) * 128, 128), 128)
            lhs[i, half, 0:B, lanes] = jnp.concatenate([high, free], axis=1)
            lhs[i, half, B:2 * B, lanes] = jnp.concatenate([low, free], axis=1)

    def right_side(slots, i, half, h, g4):
        store = near if half == 0 else far
        block_row = first_row + i
        group = h * QUAD + g4
        wanted = {s: held(block_row, zl, s) for s in slots}
        for t in range(SLOTS):
            col = held(block_row, group, t)
            inner = jnp.maximum(col, 0)
            cols = [held(group * WIDTH + inner, zl, u) for u in range(SLOTS)]
            depth = pl.ds(pl.multiple_of((g4 * SLOTS + t) * 128, 128), B)
            for s in slots:
                want = jnp.where(col >= 0, wanted[s] + 1, 0)
                hits = [jnp.where(cols[u] + 1 == want, 1, 0) * jnp.where(want > 0, 1, 0) for u in range(SLOTS)]
                u = jnp.minimum(hits[1] + 2 * hits[2], SLOTS - 1)
                on = jnp.minimum(hits[0] + hits[1] + hits[2], 1).astype(jnp.float32)
                block = store[inner & 1, (inner >> 1) & 1, g4, inner >> 2, u] * on
                high, low = split(unpack(block))
                rhs_hi[i, half, depth, s * 128:s * 128 + B] = high
                rhs_lo[i, half, depth, s * 128:s * 128 + B] = low

    def multiply(slots, i, half, added=()):
        dot = functools.partial(jnp.dot, preferred_element_type=jnp.float32)
        lanes = slice(slots[0] * 128, (slots[-1] + 1) * 128)
        main = dot(lhs[i, half], rhs_hi[i, half, :, lanes])
        rest = dot(lhs[i, half, 0:B, :], rhs_lo[i, half, :, lanes])
        value = main[0:B] + (main[B:] + rest)
        for n, s in enumerate(slots):
            part = value[:, n * 128:n * 128 + B]
            if s in added:
                out_ref[i, 0, s] += part
            else:
                out_ref[i, 0, s] = part

    def prepare():
        for ref in (rhs_hi, rhs_lo):
            for i in range(2):
                for half in range(2):
                    for n in range(QUAD * SLOTS):
                        ref[i, half, n * 128 + B:(n + 1) * 128, :] = jnp.zeros((128 - B, SLOTS * 128), jnp.bfloat16)

    def every(fn, half, h):
        def step(n, _):
            fn(n // QUAD, half, h, n % QUAD)
            return 0
        lax.fori_loop(0, 2 * QUAD, step, 0)

    diagonal = lax.axis_index("row") == lax.axis_index("col")
    holds = zh == zl // NX
    n_yk = NY * NK
    mine = y * NK + k

    def plane_copy(j):
        dx, t = (2, 1, 3, 0)[j // n_yk], (mine + j % n_yk) % n_yk
        to = {"x": (x + dx) % NX, "y": t // NK, "k": t % NK, "zh": zh, "zl": zl}
        return pltpu.make_async_remote_copy(
            src_ref=one, dst_ref=in_plane.at[mine], send_sem=out_sem.at[5], recv_sem=small_in.at[0],
            device_id=device(to), device_id_type=MESH)

    plane_copies = [plane_copy(j) for j in range(NX * n_yk) if j != 3 * n_yk]
    z_copies = {j: pltpu.make_async_remote_copy(
        src_ref=two, dst_ref=along.at[zl], send_sem=out_sem.at[6], recv_sem=small_in.at[1],
        device_id=device(moved(me, "z", j)), device_id_type=MESH)
        for j in sorted(range(1, NZ), key=lambda j: -min(j, NZ - j))}

    def diagonal_sum():
        eye = lax.broadcasted_iota(jnp.int32, (B, B), 0) == lax.broadcasted_iota(jnp.int32, (B, B), 1)
        total = jnp.sum(jnp.where(eye, out_ref[0, 0, 0] + out_ref[1, 0, 0], 0.0))
        return jnp.full((8, 128), total, jnp.float32)

    def to_plane():
        for copy in plane_copies:
            copy.start()
        in_plane[mine] = one[...]

    def to_line():
        drain(small_in.at[0], ruler.at[pl.ds(0, n_yk)], jnp.logical_not(diagonal))
        drain(small_in.at[0], ruler.at[pl.ds(0, n_yk - 1)], diagonal)
        two[...] = jnp.sum(in_plane[...], axis=0)
        for copy in z_copies.values():
            copy.start()
        along[zl] = two[...]

    other = 1 - zh
    first, rest, whole = (0,), (1, 2), (0, 1, 2)

    def early_trace():
        @pl.when(diagonal)
        def _():
            every(left_side, 0, zh)
            for i in range(2):
                multiply(first, i, 0)
            near_sum[...] = diagonal_sum()

            @pl.when(zh == 1)
            def _():
                one[...] = near_sum[...]
                to_plane()

    events.append((0.3, prepare))
    events.append((AT_NEAR, lambda: every(functools.partial(right_side, whole), 0, zh)))
    events.append((AT_TRACE, early_trace))
    events.append((AT_TRACE + 3.0, lambda: pl.when(jnp.logical_and(holds, zh == 1))(to_line)))
    events.append((AT_LEFT, lambda: every(left_side, 1, other)))
    for _, step in sorted(events, key=lambda e: e[0]):
        step()

    every(functools.partial(right_side, first), 1, other)
    for i in range(2):
        multiply(first, i, 1)

    @pl.when(jnp.logical_and(diagonal, zh == 0))
    def _():
        one[...] = 2.0 * diagonal_sum() + near_sum[...]
        to_plane()

    every(left_side, 0, zh)
    for i in range(2):
        multiply(whole, i, 0, added=first)
    every(functools.partial(right_side, rest), 1, other)
    for i in range(2):
        multiply(rest, i, 1, added=rest)
    pl.when(jnp.logical_and(holds, zh == 0))(to_line)

    drain(small_in.at[1], ruler.at[pl.ds(0, NZL)], jnp.logical_not(holds))
    drain(small_in.at[1], ruler.at[pl.ds(0, NZL - 1)], holds)
    trace_ref[0, 0] = jnp.sum(along[:, 0:1, 0:1])

    drain(out_sem.at[5], ruler.at[pl.ds(0, NX * n_yk - 1)], diagonal)
    drain(out_sem.at[6], ruler.at[pl.ds(0, NZ - 1)], holds)
    drain(out_sem.at[0], line.at[pl.ds(0, LEAPS)])
    for sem, view, when in after:
        drain(sem, view, when)


def square(table, blocks, collective_id=0, name="square"):
    return pl.pallas_call(
        kernel,
        out_shape=(jax.ShapeDtypeStruct((2, 1, SLOTS, B, B), jnp.float32), jax.ShapeDtypeStruct((1, 1), jnp.float32)),
        in_specs=[pl.BlockSpec(memory_space=pltpu.SMEM), pl.BlockSpec(memory_space=pltpu.VMEM)],
        out_specs=(pl.BlockSpec(memory_space=pltpu.VMEM), pl.BlockSpec(memory_space=pltpu.SMEM)),
        scratch_shapes=[
            pltpu.VMEM((2, SLOTS, PACK, 128), jnp.float32),
            pltpu.VMEM((NZ, 2, SLOTS, PACK, 128), jnp.float32),
            pltpu.VMEM((2, NK, NX, NY, SLOTS, PACK, 128), jnp.float32),
            pltpu.VMEM((2, NK, NX, NY, SLOTS, PACK, 128), jnp.float32),
            pltpu.VMEM((2, 2, 2 * B, DEPTH), jnp.bfloat16),
            pltpu.VMEM((2, 2, DEPTH, SLOTS * 128), jnp.bfloat16),
            pltpu.VMEM((2, 2, DEPTH, SLOTS * 128), jnp.bfloat16),
            pltpu.VMEM((NY * NK, 8, 128), jnp.float32),
            pltpu.VMEM((NZL, 8, 128), jnp.float32),
            pltpu.VMEM((8, 128), jnp.float32),
            pltpu.VMEM((8, 128), jnp.float32),
            pltpu.VMEM((8, 128), jnp.float32),
            pltpu.VMEM((NX * NY * NK, 8, 128), jnp.float32),
            pltpu.SemaphoreType.DMA((3,)),
            pltpu.SemaphoreType.DMA((2, LEAPS, SLOTS)),
            pltpu.SemaphoreType.DMA((2, LEAPS)),
            pltpu.SemaphoreType.DMA((2, NZL - 1, SLOTS)),
            pltpu.SemaphoreType.DMA((2, 2, 11)),
            pltpu.SemaphoreType.DMA((2,)),
            pltpu.SemaphoreType.DMA((2,)),
            pltpu.SemaphoreType.DMA((7,)),
            pltpu.SemaphoreType.DMA((2, LEAPS)),
            pltpu.SemaphoreType.DMA((2, NZL - 1)),
        ],
        compiler_params=pltpu.CompilerParams(collective_id=collective_id, has_side_effects=True, vmem_limit_bytes=48 << 20),
        name=name,
    )(table, blocks)


def body(blocks, block_cols, occupancy):
    table = jnp.where(occupancy == 1, block_cols, -1).transpose(2, 1, 0).reshape(-1)
    product, trace = square(table, blocks)
    return product, trace[0, 0]


def solution(mesh):
    in_specs = (P(("row", "layer"), "col", None, None, None), P(), P())
    out_specs = (P(("row", "layer"), "col", None, None, None), P())
    return jax.shard_map(body, mesh=mesh, in_specs=in_specs, out_specs=out_specs, check_vma=False)
```
